128 devices in a mesh: lat: 8 (over z_lo, y), lon: 16 (over z_hi, x, core).
Axes of the slice: x: 4, y: 4, z: 4 (z_hi: 2, z_lo: 2; z = z_hi * 2 + z_lo), core: 2. Of those that a mesh axis runs over, the one named last changes fastest.
Arguments:
- level_slabs: bfloat16 [8, 96, 768, 512], P('lat', 'lon'), may hold values from -6 to 6
- surf_tokens: bfloat16 [96, 768, 512], P('lat', 'lon'), may hold values from -6 to 6
- level_order: int32 [8], replicated, may hold values from 0 to 7, each once
- level_embed: bfloat16 [8, 512], replicated, may hold values from -6 to 6
- kv_gain: float32 [512], replicated, may hold values from 0.1 to 1.9
- latent_queries: bfloat16 [3, 512], replicated
- w_key: bfloat16 [512, 512], replicated, may hold values from -0.25 to 0.25
- w_value: bfloat16 [512, 512], replicated, may hold values from -0.25 to 0.25
- w_merge: bfloat16 [512, 512], replicated, may hold values from -0.25 to 0.25
- attn_gain: float32 [512], replicated, may hold values from 0.1 to 1.9
- w_qkv: bfloat16 [512, 1536], replicated
- w_out: bfloat16 [512, 512], replicated, may hold values from -0.25 to 0.25
- mlp_gain: float32 [512], replicated, may hold values from 0.1 to 1.9
- w_up: bfloat16 [512, 2048], replicated, may hold values from -0.25 to 0.25
- w_down: bfloat16 [2048, 512], replicated, may hold values from -0.125 to 0.125
- window_shift: int32 [2, 2], replicated, may hold values from 1 to 6, as said below
Outputs:
- blended: bfloat16 [4, 96, 768, 512], P(None, 'lat', 'lon')
The draws below stay inside these ranges and needn't reach their ends.
Inputs may be any that keep to these rules, and one draw needn't show every extreme that they name: window_shift[b] holds block b's shift along latitude, 1 to 3, and along longitude, 1 to 6; in every draw some block has both at their largest.
All inputs are finite; a program needn't handle non-finite values.
Results may differ from the reference program's by a relative error of at most 0.015.
Values may be sent and summed in bfloat16 or wider, within the bound.
A program may use at most 192 MiB of HBM per device.

```python
import math
import jax
import jax.numpy as jnp
from jax import lax

D = 512
HEADS = 16
FF = 2048
LATENT = 4
DEPTH_WIN = 2
WIN_LAT = 6
WIN_LON = 12
ATMOS = 3
LEVELS = 8
PLAT = 96
PLON = 768


def draw_latent_queries(key, part):
    key = jax.random.fold_in(key, 11)
    values = jax.random.normal(key, (ATMOS, D), jnp.float32)
    return values.astype(jnp.bfloat16)


def draw_w_qkv(key, part):
    key = jax.random.fold_in(key, 12)
    values = jax.random.normal(key, (D, 3 * D), jnp.float32)
    return (values * D ** (-0.5)).astype(jnp.bfloat16)


def draw_window_shift(key, part):
    key = jax.random.fold_in(key, 13)
    key_pick, key_lat, key_lon = jax.random.split(key, 3)
    blocks = LATENT // DEPTH_WIN
    chosen = jax.random.randint(key_pick, (), 0, blocks)
    shift_lat = jax.random.randint(key_lat, (blocks,), 1, WIN_LAT // 2 + 1)
    shift_lon = jax.random.randint(key_lon, (blocks,), 1, WIN_LON // 2 + 1)
    block_ids = jnp.arange(blocks, dtype=jnp.int32)
    shift_lat = jnp.where(block_ids == chosen, WIN_LAT // 2, shift_lat)
    shift_lon = jnp.where(block_ids == chosen, WIN_LON // 2, shift_lon)
    return jnp.stack([shift_lat, shift_lon], 1).astype(jnp.int32)


def shard_levels(own_key, extent, cuts, smallest, high):
    factor_of, own = 1.0, jax.random.fold_in(own_key, 6)
    for axis_at, shards_of in cuts:
        draws = jnp.exp(jax.random.uniform(jax.random.fold_in(own, axis_at), (shards_of,), jnp.float32, smallest / len(cuts), high / len(cuts)))
        factor_of = factor_of * jnp.repeat(draws, extent[axis_at] // shards_of).reshape([-1 if axis == axis_at else 1 for axis in range(len(extent))])
    return factor_of


def bell_draw(key, extent, scale, most, cuts=(), held_as=jnp.bfloat16):
    drawn = scale * jax.random.normal(key, extent, jnp.float32)
    if cuts:
        drawn = drawn * shard_levels(key, extent, cuts, -0.22, 0.18)
    return jnp.clip(drawn, -most, most).astype(held_as)


def setup_inputs(seed: int = 0) -> dict:
    key_of = jax.random.split(jax.random.key(seed), 17)
    level_slabs = bell_draw(key_of[0], (LEVELS, PLAT, PLON, D), 1.0, 6.0, ((0, 8), (1, 16)))
    surf_tokens = bell_draw(key_of[1], (PLAT, PLON, D), 1.0, 6.0, ((0, 8), (1, 16)))
    level_order = jax.random.permutation(key_of[2], LEVELS).astype(jnp.int32)
    level_embed = bell_draw(key_of[3], (LEVELS, D), 1.0, 6.0)
    kv_gain = jnp.clip(1.0 + 0.18 * jax.random.normal(key_of[4], (D,), jnp.float32), 0.1, 1.9)
    latent_queries = draw_latent_queries(jax.random.fold_in(key_of[16], 71), 0)
    w_key = bell_draw(key_of[6], (D, D), D ** -0.5, 0.25)
    w_value = bell_draw(key_of[7], (D, D), D ** -0.5, 0.25)
    w_merge = bell_draw(key_of[8], (D, D), D ** -0.5, 0.25)
    attn_gain = jnp.clip(1.0 + 0.18 * jax.random.normal(key_of[9], (D,), jnp.float32), 0.1, 1.9)
    w_qkv = draw_w_qkv(jax.random.fold_in(key_of[16], 71), 0)
    w_out = bell_draw(key_of[11], (D, D), D ** -0.5, 0.25)
    mlp_gain = jnp.clip(1.0 + 0.18 * jax.random.normal(key_of[12], (D,), jnp.float32), 0.1, 1.9)
    w_up = bell_draw(key_of[13], (D, FF), D ** -0.5, 0.25)
    w_down = bell_draw(key_of[14], (FF, D), FF ** -0.5, 0.125)
    window_shift = draw_window_shift(jax.random.fold_in(key_of[16], 71), 0)
    return {"level_slabs": level_slabs, "surf_tokens": surf_tokens, "level_order": level_order, "level_embed": level_embed, "kv_gain": kv_gain, "latent_queries": latent_queries, "w_key": w_key, "w_value": w_value, "w_merge": w_merge, "attn_gain": attn_gain, "w_qkv": w_qkv, "w_out": w_out, "mlp_gain": mlp_gain, "w_up": w_up, "w_down": w_down, "window_shift": window_shift}


def layer_norm(values_in, gain_vec):
    row_mean = lax.optimization_barrier(jnp.mean(values_in, axis=-1, keepdims=True))
    centred = values_in - row_mean
    variance = lax.optimization_barrier(jnp.mean(centred * centred, axis=-1, keepdims=True))
    return centred * lax.rsqrt(variance + 1e-05) * gain_vec

def perceive(slab_rows, embed_rows, kv_gain, latent_queries, w_key, w_value, w_merge):
    levels, patches, features = slab_rows.shape
    head_size = features // HEADS
    query_count = latent_queries.shape[0]
    tokens = slab_rows.astype(jnp.float32) + embed_rows[:, None, :]
    normed = layer_norm(tokens, kv_gain.astype(jnp.float32)).astype(jnp.bfloat16).reshape(levels * patches, features)
    key_rows = jnp.dot(normed, w_key, preferred_element_type=jnp.float32).astype(jnp.bfloat16)
    value_rows = jnp.dot(normed, w_value, preferred_element_type=jnp.float32).astype(jnp.bfloat16)
    key_rows = key_rows.reshape(levels, patches, HEADS, head_size).astype(jnp.float32)
    value_rows = value_rows.reshape(levels, patches, HEADS, head_size).astype(jnp.float32)
    queries = latent_queries.reshape(query_count, HEADS, head_size).astype(jnp.float32)
    scores = jnp.einsum('ahe,lnhe->nhal', queries, key_rows) / math.sqrt(head_size)
    weights = jax.nn.softmax(scores, axis=-1).astype(jnp.bfloat16)
    attended = jnp.einsum('nhal,lnhe->anhe', weights.astype(jnp.float32), value_rows).astype(jnp.bfloat16)
    attended = attended.reshape(query_count * patches, features)
    merged = jnp.dot(attended, w_merge, preferred_element_type=jnp.float32).reshape(query_count, patches, features)
    merged = merged + latent_queries.astype(jnp.float32)[:, None, :]
    return merged.astype(jnp.bfloat16)

def to_windows(tensor_in):
    depth, tile_rows, tile_cols = tensor_in.shape[:3]
    rest = tensor_in.shape[3:]
    shaped = tensor_in.reshape((depth, tile_rows // WIN_LAT, WIN_LAT, tile_cols // WIN_LON, WIN_LON) + rest)
    moved = shaped.transpose((1, 3, 0, 2, 4) + tuple(range(5, 5 + len(rest))))
    return moved.reshape((tile_rows // WIN_LAT, tile_cols // WIN_LON, depth * WIN_LAT * WIN_LON) + rest)

def from_windows(tensor_in, depth_blocks, grid_lat, grid_lon):
    features = tensor_in.shape[-1]
    shaped = tensor_in.reshape(depth_blocks, grid_lat, grid_lon, DEPTH_WIN, WIN_LAT, WIN_LON, features)
    moved = shaped.transpose(0, 3, 1, 4, 2, 5, 6)
    return moved.reshape(depth_blocks * DEPTH_WIN, grid_lat * WIN_LAT, grid_lon * WIN_LON, features)

def window_attention(windows, region, attn_gain, w_qkv, w_out):
    batch, span, features = windows.shape
    head_size = features // HEADS
    normed = layer_norm(windows.astype(jnp.float32), attn_gain.astype(jnp.float32)).astype(jnp.bfloat16)
    projected = jnp.dot(normed.reshape(batch * span, features), w_qkv, preferred_element_type=jnp.float32)
    projected = projected.astype(jnp.bfloat16).reshape(batch, span, 3, HEADS, head_size).astype(jnp.float32)
    scores = jnp.einsum('bqhe,bkhe->bhqk', projected[:, :, 0], projected[:, :, 1]) / math.sqrt(head_size)
    allowed = region[:, :, None] == region[:, None, :]
    scores = jnp.where(allowed[:, None], scores, -1e+30)
    weights = jax.nn.softmax(scores, axis=-1).astype(jnp.bfloat16)
    attended = jnp.einsum('bhqk,bkhe->bqhe', weights.astype(jnp.float32), projected[:, :, 2]).astype(jnp.bfloat16)
    attended = attended.reshape(batch * span, features)
    summed = windows.astype(jnp.float32).reshape(batch * span, features) + jnp.dot(attended, w_out, preferred_element_type=jnp.float32)
    return summed.astype(jnp.bfloat16).reshape(batch, span, features)

def feed_forward(rows_in, mlp_gain, w_up, w_down):
    normed = layer_norm(rows_in.astype(jnp.float32), mlp_gain.astype(jnp.float32)).astype(jnp.bfloat16)
    hidden_units = jax.nn.gelu(jnp.dot(normed, w_up, preferred_element_type=jnp.float32)).astype(jnp.bfloat16)
    summed = rows_in.astype(jnp.float32) + jnp.dot(hidden_units, w_down, preferred_element_type=jnp.float32)
    return summed.astype(jnp.bfloat16)

def reference(level_slabs, surf_tokens, level_order, level_embed, kv_gain, latent_queries, w_key, w_value, w_merge, attn_gain, w_qkv, w_out, mlp_gain, w_up, w_down, window_shift):
    features = level_slabs.shape[-1]
    picker = (level_order[:, None] == jnp.arange(LEVELS, dtype=jnp.int32)[None, :]).astype(jnp.float32)
    embed_rows = jnp.dot(picker, level_embed.astype(jnp.float32), precision=lax.Precision.HIGHEST)
    by_rows = jnp.moveaxis(level_slabs, 1, 0)

    def aggregate(slab_row):
        return perceive(slab_row, embed_rows, kv_gain, latent_queries, w_key, w_value, w_merge)
    atmosphere = jnp.moveaxis(lax.map(aggregate, by_rows), 0, 1)
    latent = jnp.concatenate([surf_tokens[None], atmosphere], 0)
    outputs = []
    for block_id in range(LATENT // DEPTH_WIN):
        shift_lat = window_shift[block_id, 0]
        shift_lon = window_shift[block_id, 1]
        segment = latent[block_id * DEPTH_WIN:(block_id + 1) * DEPTH_WIN]
        rolled = jnp.roll(segment, (-shift_lat, -shift_lon), axis=(1, 2))
        region = (jnp.arange(PLAT, dtype=jnp.int32) >= PLAT - shift_lat).astype(jnp.int32)
        region_grid = jnp.broadcast_to(region[None, :, None, None], (DEPTH_WIN, PLAT, PLON, 1))
        windows = to_windows(rolled)
        region_windows = to_windows(region_grid)[..., 0]

        def one_row(pair):
            win_row, reg_row = pair
            attended = window_attention(win_row, reg_row, attn_gain, w_qkv, w_out)
            fed = feed_forward(attended.reshape(-1, features), mlp_gain, w_up, w_down)
            return fed.reshape(attended.shape)
        mixed_rows = lax.map(one_row, (windows, region_windows))
        restored = from_windows(mixed_rows.reshape(-1, DEPTH_WIN * WIN_LAT * WIN_LON, features), 1, PLAT // WIN_LAT, PLON // WIN_LON)
        outputs.append(jnp.roll(restored, (shift_lat, shift_lon), axis=(1, 2)))
    return jnp.concatenate(outputs, 0)
```

```python
import functools
import math

import jax
import jax.numpy as jnp
import numpy as np
from jax import lax
from jax.experimental import pallas as pl
from jax.experimental.pallas import tpu as pltpu
from jax.sharding import PartitionSpec as P

D = 512
HEADS = 16
HEAD = D // HEADS
FF = 2048
ATMOS = 3
LATENT = 4
WIN_LAT = 6
WIN_LON = 12
SPAN = 2 * WIN_LAT * WIN_LON
ROWS = 12
COLS = 48
GRP = 16
GROUPS = COLS // GRP
HALO = 3
PATCHES = WIN_LAT * GRP
BATCH = 4 * SPAN
LANES = 128
LOG2E = math.log2(math.e)
MESH = pl.DeviceIdType.MESH
F32 = jnp.float32
BF16 = jnp.bfloat16
BASES = (0, 0, 16, 32)
OFFSETS = (0, 12, 8, 4)


def dot(a, b):
    return jnp.dot(a, b, preferred_element_type=F32)


def norm(x, gain):
    mean = jnp.mean(x, axis=-1, keepdims=True)
    centred = x - mean
    variance = jnp.mean(centred * centred, axis=-1, keepdims=True)
    return (centred * lax.rsqrt(variance + 1e-05) * gain).astype(BF16)


def gelu(x):
    c = math.sqrt(2.0 / math.pi)
    return 0.5 * x * (1.0 + jnp.tanh(x * (c + (c * 0.044715) * (x * x))))


def kernel(
    lats,
    lons,
    order_ref,
    shift_ref,
    slabs,
    surf,
    embed_ref,
    kv_gain_ref,
    queries_ref,
    attn_gain_ref,
    mlp_gain_ref,
    to_cells_ref,
    from_cells_ref,
    w_key,
    w_value,
    w_merge,
    w_qkv,
    w_out,
    w_up,
    w_down,
    out,
    recv,
    latent,
    result,
    from_north,
    from_west,
    from_corner,
    key_v,
    value_v,
    merge_v,
    qkv_v,
    out_v,
    up_v,
    down_v,
    embed_v,
    fold_v,
    value_p,
    merge_p,
    normed_v,
    values_v,
    scores_v,
    mix_v,
    x_v,
    q_v,
    k_v,
    v_v,
    attended_v,
    y_v,
    send_sem,
    recv_sem,
    weight_sem,
    halo_send,
    halo_recv,
    back_send,
    back_recv,
    out_sem,
):
    la = lax.axis_index("lat")
    lo = lax.axis_index("lon")
    north = lax.rem(la + lats - 1, lats)
    south = lax.rem(la + 1, lats)
    west = lax.rem(lo + lons - 1, lons)
    east = lax.rem(lo + 1, lons)
    half = lax.rem(lo, 2)
    dest_lat = lo // 2
    has_self = dest_lat == la

    def is_self(lat, lon):
        return jnp.logical_and(lat == la, lon == lo)

    barrier = pltpu.get_barrier_semaphore()

    def greet(lat, lon):
        pl.semaphore_signal(barrier, inc=1, device_id=(lat, lon), device_id_type=MESH)

    for lat in range(lats):
        for r in range(2):
            lon = 2 * la + r

            @pl.when(jnp.logical_not(is_self(lat, lon)))
            def _():
                greet(lat, lon)

    for lat, lon in ((south, lo), (la, east), (south, east), (north, lo), (la, west), (north, west)):
        greet(lat, lon)
    pl.semaphore_wait(barrier, 6 + 2 * lats - jnp.where(has_self, 1, 0))

    def part_copy(g, k):
        lon = lax.rem(2 * la + half + k, lons)
        source = slabs.at[0, :, pl.ds(pl.multiple_of(lon * COLS + g * GRP, GRP), GRP), :]
        target = recv.at[g, half, la]
        return lon, source, target

    def send(i, carry):
        g, k = i // lons, lax.rem(i, lons)
        lon, source, target = part_copy(g, k)

        @pl.when(is_self(dest_lat, lon))
        def _():
            pltpu.make_async_copy(source, target, recv_sem.at[g, half, la]).start()

        @pl.when(jnp.logical_not(is_self(dest_lat, lon)))
        def _():
            pltpu.make_async_remote_copy(
                source,
                target,
                send_sem.at[g, k],
                recv_sem.at[g, half, la],
                device_id=(dest_lat, lon),
                device_id_type=MESH,
            ).start()

        return carry

    lax.fori_loop(0, GROUPS * lons, send, 0)

    loads = [
        pltpu.make_async_copy(source, target, weight_sem.at[i])
        for i, (source, target) in enumerate(
            (
                (w_key, key_v),
                (w_value, value_v),
                (w_merge, merge_v),
                (w_qkv, qkv_v),
                (w_out, out_v),
                (w_up, up_v),
                (w_down, down_v),
                (surf, latent.at[0, pl.ds(0, ROWS), pl.ds(0, COLS), :]),
            )
        )
    ]
    for load in loads:
        load.start()
    result[...] = jnp.zeros_like(result)
    embed_v[...] = embed_ref[...].astype(F32)

    new = lax.broadcasted_iota(jnp.int32, (D, D), 1)
    old = lax.broadcasted_iota(jnp.int32, (D, D), 0)
    loads[1].wait()
    value_p[...] = dot(
        value_v[...], jnp.where(old == (new % HEADS) * HEAD + new // HEADS, 1.0, 0.0).astype(BF16)
    ).astype(BF16)
    loads[2].wait()
    merge_p[...] = dot(
        jnp.where(new == (old % HEADS) * HEAD + old // HEADS, 1.0, 0.0).astype(BF16), merge_v[...]
    ).astype(BF16)
    loads[0].wait()
    head_of = lax.broadcasted_iota(jnp.int32, (LANES, D), 1) // HEAD
    row_head = lax.broadcasted_iota(jnp.int32, (LANES, D), 0) % HEADS
    for a in range(ATMOS):
        picked = jnp.where(head_of == row_head, queries_ref[a : a + 1, :].astype(F32), 0.0).astype(BF16)
        folded = lax.dot_general(
            picked, key_v[...], (((1,), (1,)), ((), ())), preferred_element_type=F32
        )
        folded = folded.T * (LOG2E / math.sqrt(HEAD))
        high = folded.astype(BF16)
        fold_v[:, a * LANES : (a + 1) * LANES] = high
        fold_v[:, (ATMOS + a) * LANES : (ATMOS + a + 1) * LANES] = (folded - high.astype(F32)).astype(BF16)

    def aggregate(g, h):
        def one_level(j, carry):
            landed = recv.at[g, h, j]
            pltpu.make_async_copy(landed, landed, recv_sem.at[g, h, j]).wait()
            row = embed_v[pl.ds(order_ref[j], 1), :]
            x = landed[...].reshape(PATCHES, D).astype(F32) + row
            normed_v[pl.ds(pl.multiple_of(j * PATCHES, PATCHES), PATCHES), :] = norm(x, kv_gain_ref[...])
            return carry

        lax.fori_loop(0, lats, one_level, 0)
        values_v[...] = dot(normed_v[...], value_p[...]).astype(BF16)
        scores_v[...] = dot(normed_v[...], fold_v[:, : ATMOS * LANES]) + dot(
            normed_v[...], fold_v[:, ATMOS * LANES :]
        )
        for a in range(ATMOS):
            cut = slice(a * LANES, (a + 1) * LANES)
            level = [scores_v[j * PATCHES : (j + 1) * PATCHES, cut] for j in range(lats)]
            top = functools.reduce(jnp.maximum, level)
            level = [jnp.exp2(s - top) for s in level]
            scale = 1.0 / functools.reduce(jnp.add, level)
            level = [e * scale for e in level]
            for c in range(D // LANES):
                lanes = slice(c * LANES, (c + 1) * LANES)
                mixed = functools.reduce(
                    jnp.add,
                    [
                        level[j] * values_v[j * PATCHES : (j + 1) * PATCHES, lanes].astype(F32)
                        for j in range(lats)
                    ],
                )
                mix_v[a * PATCHES : (a + 1) * PATCHES, lanes] = mixed.astype(BF16)
        merged = dot(mix_v[...], merge_p[...])
        for a in range(ATMOS):
            tokens = merged[a * PATCHES : (a + 1) * PATCHES] + queries_ref[a : a + 1, :].astype(F32)
            latent[
                1 + a, pl.ds(pl.multiple_of(h * WIN_LAT, WIN_LAT), WIN_LAT), g * GRP : (g + 1) * GRP, :
            ] = tokens.astype(BF16).reshape(WIN_LAT, GRP, D)

    def aggregate_group(g):
        lax.fori_loop(0, 2, lambda h, carry: (aggregate(g, h), carry)[1], 0)

    def halo(i, rows, cols, to_rows, to_cols, lat, lon):
        return pltpu.make_async_remote_copy(
            latent.at[:, pl.ds(rows, to_rows[1]), pl.ds(cols, GRP), :],
            latent.at[:, pl.ds(to_rows[0], to_rows[1]), pl.ds(to_cols, GRP), :],
            halo_send.at[i],
            halo_recv.at[i],
            device_id=(lat, lon),
            device_id_type=MESH,
        )

    row_halos = [
        halo(g, 0, g * GRP, (ROWS, HALO), g * GRP, north, lo) for g in range(GROUPS)
    ]
    col_halo = halo(GROUPS, 0, 0, (0, ROWS), COLS, la, west)
    corner_halo = halo(GROUPS + 1, 0, 0, (ROWS, HALO), COLS, north, west)

    last = la == lats - 1

    def attend(pair, rw):
        first_row = rw * WIN_LAT + 1
        windows = [(b, 2 * pair + c) for b in range(2) for c in range(2)]
        for w, (b, cw) in enumerate(windows):
            place = (shift_ref[b, 0] - 1) * 32 + shift_ref[b, 1] + OFFSETS[cw]
            cells = latent[2 * b : 2 * b + 2, pl.ds(first_row, 8), BASES[cw] : BASES[cw] + 32, :]
            at = lax.broadcasted_iota(jnp.int32, (SPAN, 512), 1)
            pick = jnp.where(at == to_cells_ref[...] + place, 1.0, 0.0).astype(BF16)
            x_v[w * SPAN : (w + 1) * SPAN, :] = dot(pick, cells.reshape(512, D))
        normed = norm(x_v[...], attn_gain_ref[...])
        q_v[...] = (dot(normed, qkv_v[:, :D]) * (LOG2E / math.sqrt(HEAD))).astype(BF16)
        k_v[...] = dot(normed, qkv_v[:, D : 2 * D]).astype(BF16)
        v_v[...] = dot(normed, qkv_v[:, 2 * D :]).astype(BF16)
        lane_head = lax.broadcasted_iota(jnp.int32, (SPAN, LANES), 1) // HEAD
        ones = jnp.ones((SPAN, LANES), BF16)
        row_of_q = lax.broadcasted_iota(jnp.int32, (SPAN, SPAN), 0)
        row_of_k = lax.broadcasted_iota(jnp.int32, (SPAN, SPAN), 1)
        row_of_q = (row_of_q // WIN_LON) % WIN_LAT
        row_of_k = (row_of_k // WIN_LON) % WIN_LAT
        edge = jnp.where(jnp.logical_and(last, rw == 1), 0, WIN_LAT)

        def window(w, carry):
            at = pl.ds(pl.multiple_of(w * SPAN, 16), SPAN)
            start = WIN_LAT - shift_ref[w // 2, 0] + edge
            bias = jnp.where((row_of_q >= start) == (row_of_k >= start), 0.0, -1e30)
            for c in range(D // LANES):
                lanes = slice(c * LANES, (c + 1) * LANES)
                q = q_v[at, lanes]
                k = k_v[at, lanes]
                v = jnp.concatenate([v_v[at, lanes], ones], axis=1)
                mixed = jnp.zeros((SPAN, LANES), F32)
                for h in range(LANES // HEAD):
                    own = lane_head == h
                    s = lax.dot_general(
                        jnp.where(own, q, jnp.zeros_like(q)),
                        k,
                        (((1,), (1,)), ((), ())),
                        preferred_element_type=F32,
                    )
                    s = s + bias
                    p = jnp.exp2(s - jnp.max(s, axis=-1, keepdims=True)).astype(BF16)
                    o = dot(p, v)
                    mixed = jnp.where(own, o[:, :LANES] / o[:, LANES:], mixed)
                attended_v[at, lanes] = mixed.astype(BF16)
            return carry

        lax.fori_loop(0, 4, window, 0)
        first = (x_v[...] + dot(attended_v[...], out_v[...])).astype(BF16).astype(F32)
        normed = norm(first, mlp_gain_ref[...])
        total = first
        for c in range(FF // 512):
            cut = slice(c * 512, (c + 1) * 512)
            hidden = gelu(dot(normed, up_v[:, cut])).astype(BF16)
            total = total + dot(hidden, down_v[cut, :])
        y_v[...] = total.astype(BF16)
        for w, (b, cw) in enumerate(windows):
            place = (shift_ref[b, 0] - 1) * 32 + shift_ref[b, 1] + OFFSETS[cw]
            at = lax.broadcasted_iota(jnp.int32, (512, SPAN), 0)
            put = jnp.where(at == from_cells_ref[0:1, :] + place, 1.0, 0.0).astype(BF16)
            moved = dot(put, y_v[w * SPAN : (w + 1) * SPAN, :]).astype(BF16).reshape(2, 8, 32, D)
            where = (slice(2 * b, 2 * b + 2), pl.ds(first_row, 8), slice(BASES[cw], BASES[cw] + 32))
            result[where] = result[where] + moved

    def back(i, source, target, lat, lon):
        return pltpu.make_async_remote_copy(
            source, target, back_send.at[i], back_recv.at[i], device_id=(lat, lon), device_id_type=MESH
        )

    backs = (
        back(0, result.at[:, pl.ds(ROWS, HALO), pl.ds(0, COLS), :], from_north, south, lo),
        back(1, result.at[:, pl.ds(0, ROWS), pl.ds(COLS, GRP), :], from_west, la, east),
        back(2, result.at[:, pl.ds(ROWS, HALO), pl.ds(COLS, GRP), :], from_corner, south, east),
    )

    aggregate_group(0)
    loads[7].wait()
    row_halos[0].start()
    col_halo.start()
    corner_halo.start()
    aggregate_group(1)
    row_halos[1].start()
    for i in range(3, 7):
        loads[i].wait()

    def first_pair(rw, carry):
        @pl.when(rw == 1)
        def _():
            row_halos[0].wait_recv()
            row_halos[1].wait_recv()

        attend(0, rw)
        return carry

    lax.fori_loop(0, 2, first_pair, 0)
    aggregate_group(2)
    row_halos[2].start()

    def second_pair(rw, carry):
        @pl.when(rw == 0)
        def _():
            col_halo.wait_recv()

        @pl.when(rw == 1)
        def _():
            row_halos[2].wait_recv()
            corner_halo.wait_recv()

        attend(1, rw)
        return carry

    lax.fori_loop(0, 2, second_pair, 0)
    for copy in backs:
        copy.start()
    for copy in backs:
        copy.wait_recv()
    result[:, 0:HALO, 0:COLS, :] = result[:, 0:HALO, 0:COLS, :] + from_north[...]
    result[:, 0:ROWS, 0:GRP, :] = result[:, 0:ROWS, 0:GRP, :] + from_west[...]
    result[:, 0:HALO, 0:GRP, :] = result[:, 0:HALO, 0:GRP, :] + from_corner[...]
    done = pltpu.make_async_copy(result.at[:, pl.ds(0, ROWS), pl.ds(0, COLS), :], out, out_sem)
    done.start()
    for copy in backs:
        copy.wait_send()
    for copy in row_halos + [col_halo, corner_halo]:
        copy.wait_send()

    def sent(i, carry):
        g, k = i // lons, lax.rem(i, lons)
        lon, source, target = part_copy(g, k)

        @pl.when(jnp.logical_not(is_self(dest_lat, lon)))
        def _():
            pltpu.make_async_remote_copy(
                source,
                target,
                send_sem.at[g, k],
                recv_sem.at[g, half, la],
                device_id=(dest_lat, lon),
                device_id_type=MESH,
            ).wait_send()

        return carry

    lax.fori_loop(0, GROUPS * lons, sent, 0)
    done.wait()


def shards(
    lats,
    lons,
    level_slabs,
    surf_tokens,
    level_order,
    level_embed,
    kv_gain,
    latent_queries,
    w_key,
    w_value,
    w_merge,
    attn_gain,
    w_qkv,
    w_out,
    mlp_gain,
    w_up,
    w_down,
    window_shift,
):
    token = np.arange(SPAN)
    cell = (token // 72) * 256 + (token % 72) // 12 * 32 + token % 12
    to_cells = jnp.asarray(cell[:, None], jnp.int32)
    from_cells = jnp.asarray(np.broadcast_to(cell[None, :], (8, SPAN)), jnp.int32)
    smem = pl.BlockSpec(memory_space=pltpu.SMEM)
    vmem = pl.BlockSpec(memory_space=pltpu.VMEM)
    hbm = pl.BlockSpec(memory_space=pl.ANY)
    tokens = lats * PATCHES
    return pl.pallas_call(
        functools.partial(kernel, lats, lons),
        out_shape=jax.ShapeDtypeStruct((LATENT, ROWS, COLS, D), BF16),
        in_specs=[smem] * 2 + [hbm] * 2 + [vmem] * 7 + [hbm] * 7,
        out_specs=hbm,
        scratch_shapes=[
            pltpu.VMEM((GROUPS, 2, lats, WIN_LAT, GRP, D), BF16),
            pltpu.VMEM((LATENT, ROWS + HALO, COLS + GRP, D), BF16),
            pltpu.VMEM((LATENT, ROWS + HALO, COLS + GRP, D), BF16),
            pltpu.VMEM((LATENT, HALO, COLS, D), BF16),
            pltpu.VMEM((LATENT, ROWS, GRP, D), BF16),
            pltpu.VMEM((LATENT, HALO, GRP, D), BF16),
            pltpu.VMEM((D, D), BF16),
            pltpu.VMEM((D, D), BF16),
            pltpu.VMEM((D, D), BF16),
            pltpu.VMEM((D, 3 * D), BF16),
            pltpu.VMEM((D, D), BF16),
            pltpu.VMEM((D, FF), BF16),
            pltpu.VMEM((FF, D), BF16),
            pltpu.VMEM((lats, D), F32),
            pltpu.VMEM((D, 2 * ATMOS * LANES), BF16),
            pltpu.VMEM((D, D), BF16),
            pltpu.VMEM((D, D), BF16),
            pltpu.VMEM((tokens, D), BF16),
            pltpu.VMEM((tokens, D), BF16),
            pltpu.VMEM((tokens, ATMOS * LANES), F32),
            pltpu.VMEM((ATMOS * PATCHES, D), BF16),
            pltpu.VMEM((BATCH, D), F32),
            pltpu.VMEM((BATCH, D), BF16),
            pltpu.VMEM((BATCH, D), BF16),
            pltpu.VMEM((BATCH, D), BF16),
            pltpu.VMEM((BATCH, D), BF16),
            pltpu.VMEM((BATCH, D), BF16),
            pltpu.SemaphoreType.DMA((GROUPS, lons)),
            pltpu.SemaphoreType.DMA((GROUPS, 2, lats)),
            pltpu.SemaphoreType.DMA((8,)),
            pltpu.SemaphoreType.DMA((GROUPS + 2,)),
            pltpu.SemaphoreType.DMA((GROUPS + 2,)),
            pltpu.SemaphoreType.DMA((3,)),
            pltpu.SemaphoreType.DMA((3,)),
            pltpu.SemaphoreType.DMA,
        ],
        compiler_params=pltpu.CompilerParams(
            collective_id=0, has_side_effects=True, vmem_limit_bytes=56 * 1024 * 1024
        ),
        name="encoder",
    )(
        level_order,
        window_shift,
        level_slabs,
        surf_tokens,
        level_embed,
        kv_gain.reshape(1, D),
        latent_queries,
        attn_gain.reshape(1, D),
        mlp_gain.reshape(1, D),
        to_cells,
        from_cells,
        w_key,
        w_value,
        w_merge,
        w_qkv,
        w_out,
        w_up,
        w_down,
    )


def solution(mesh):
    in_specs = (P("lat", "lon", None, None), P("lat", "lon", None)) + (P(),) * 14
    return jax.shard_map(
        functools.partial(shards, mesh.shape["lat"], mesh.shape["lon"]),
        mesh=mesh,
        in_specs=in_specs,
        out_specs=P(None, "lat", "lon", None),
        check_vma=False,
    )
```

```python
import functools
import math

import jax
import jax.numpy as jnp
import numpy as np
from jax import lax
from jax.experimental import pallas as pl
from jax.experimental.pallas import tpu as pltpu
from jax.sharding import PartitionSpec as P

D = 512
HEADS = 16
HEAD = D // HEADS
FF = 2048
ATMOS = 3
LATENT = 4
WIN_LAT = 6
WIN_LON = 12
SPAN = 2 * WIN_LAT * WIN_LON
ROWS = 12
COLS = 48
GRP = 16
GROUPS = COLS // GRP
HALO = 3
EDGE = 8
PATCHES = WIN_LAT * GRP
BATCH = 2 * SPAN
LANES = 128
LOG2E = math.log2(math.e)
MESH = pl.DeviceIdType.MESH
F32 = jnp.float32
BF16 = jnp.bfloat16
BASES = (0, 0, 16, 32)
OFFSETS = (0, 12, 8, 4)


def dot(a, b):
    return jnp.dot(a, b, preferred_element_type=F32)


def norm(x, gain):
    mean = jnp.mean(x, axis=-1, keepdims=True)
    centred = x - mean
    variance = jnp.mean(centred * centred, axis=-1, keepdims=True)
    return (centred * lax.rsqrt(variance + 1e-05) * gain).astype(BF16)


def gelu(x):
    c = math.sqrt(2.0 / math.pi)
    return 0.5 * x * (1.0 + jnp.tanh(x * (c + (c * 0.044715) * (x * x))))


def kernel(
    lats,
    lons,
    order_ref,
    shift_ref,
    slabs,
    surf,
    embed_ref,
    kv_gain_ref,
    queries_ref,
    attn_gain_ref,
    mlp_gain_ref,
    to_cells_ref,
    from_cells_ref,
    w_key,
    w_value,
    w_merge,
    w_qkv,
    w_out,
    w_up,
    w_down,
    out,
    recv,
    relay,
    latent,
    result,
    from_north,
    from_west,
    from_corner,
    ahead_out,
    ahead_in,
    ahead_corner,
    back_out,
    key_v,
    value_v,
    merge_v,
    qkv_v,
    out_v,
    up_v,
    down_v,
    embed_v,
    fold_v,
    value_p,
    merge_p,
    normed_v,
    values_v,
    scores_v,
    mix_v,
    x_v,
    q_v,
    k_v,
    v_v,
    attended_v,
    y_v,
    send_sem,
    recv_sem,
    relay_send,
    relay_recv,
    weight_sem,
    halo_send,
    halo_recv,
    back_send,
    back_recv,
    out_sem,
):
    la = lax.axis_index("lat")
    lo = lax.axis_index("lon")
    north = lax.rem(la + lats - 1, lats)
    south = lax.rem(la + 1, lats)
    west = lax.rem(lo + lons - 1, lons)
    east = lax.rem(lo + 1, lons)
    half = lax.rem(lo, 2)
    dest_lat = lo // 2
    has_self = dest_lat == la
    half_lats, half_lons = lats // 2, lons // 2
    z_lo, z_hi = la // half_lats, lo // half_lons
    outer = z_lo == z_hi
    across = lax.rem(la + half_lats, lats)

    def is_self(lat, lon):
        return jnp.logical_and(lat == la, lon == lo)

    barrier = pltpu.get_barrier_semaphore()

    def greet(lat, lon):
        pl.semaphore_signal(barrier, inc=1, device_id=(lat, lon), device_id_type=MESH)

    for lat in range(lats):
        for r in range(2):
            lon = 2 * la + r
            by_relay = jnp.logical_and(jnp.logical_not(outer), lat // half_lats == z_lo)

            @pl.when(jnp.logical_not(jnp.logical_or(is_self(lat, lon), by_relay)))
            def _():
                greet(lat, lon)

    @pl.when(jnp.logical_not(outer))
    def _():
        greet(across, lo)

    @pl.when(outer)
    def _():
        for y in range(half_lats):
            for r in range(2):
                greet((1 - z_lo) * half_lats + y, 2 * across + r)

    for lat, lon in ((south, lo), (la, east), (south, east), (north, lo), (la, west), (north, west)):
        greet(lat, lon)
    pl.semaphore_wait(barrier, 6 + 2 * lats + jnp.where(outer, 1, 0) - jnp.where(has_self, 1, 0))

    def part_to(k):
        x = lax.rem(lax.rem(lo, half_lons) // 2 + k, half_lats)
        core = lax.rem(half + k // half_lons, 2)
        return lax.rem(z_hi + 1 + k // half_lats, 2) * half_lons + 2 * x + core

    def relayed(lon):
        return jnp.logical_and(outer, lon // half_lons != z_hi)

    def part_copies(g, k):
        lon = part_to(k)
        source = slabs.at[0, :, pl.ds(pl.multiple_of(lon * COLS + g * GRP, GRP), GRP), :]
        target = recv.at[g, half, la]
        y = lax.rem(la, half_lats)
        return (
            pltpu.make_async_copy(source, target, recv_sem.at[g, half, la]),
            pltpu.make_async_remote_copy(
                source,
                target,
                send_sem.at[g, k],
                recv_sem.at[g, half, la],
                device_id=(dest_lat, lon),
                device_id_type=MESH,
            ),
            pltpu.make_async_remote_copy(
                source,
                relay.at[g, half, y],
                send_sem.at[g, k],
                relay_recv.at[g, half, y],
                device_id=(lax.rem(dest_lat + half_lats, lats), lon),
                device_id_type=MESH,
            ),
        )

    def send_part(g, k):
        lon = part_to(k)
        own = is_self(dest_lat, lon)

        @pl.when(own)
        def _():
            part_copies(g, k)[0].start()

        @pl.when(relayed(lon))
        def _():
            part_copies(g, k)[2].start()

        @pl.when(jnp.logical_not(jnp.logical_or(own, relayed(lon))))
        def _():
            part_copies(g, k)[1].start()

    def sent_part(g, k):
        @pl.when(jnp.logical_not(is_self(dest_lat, part_to(k))))
        def _():
            part_copies(g, k)[1].wait_send()

    def relay_copy(g, h, y):
        level = (1 - z_lo) * half_lats + y
        return pltpu.make_async_remote_copy(
            relay.at[g, h, y],
            recv.at[g, h, level],
            relay_send.at[g, h, y],
            recv_sem.at[g, h, level],
            device_id=(across, lo),
            device_id_type=MESH,
        )

    def send_on(g, first):
        @pl.when(outer)
        def _():
            h = half if first else 1 - half

            def step(y, carry):
                landed = relay.at[g, h, y]
                pltpu.make_async_copy(landed, landed, relay_recv.at[g, h, y]).wait()
                relay_copy(g, h, y).start()
                return carry

            lax.fori_loop(0, half_lats, step, 0)

    def next_group(g):
        def step(k, carry):
            sent_part(g, k)
            send_part(g + 1, k)
            return carry

        lax.fori_loop(0, lons // 2, step, 0)
        send_on(g, True)
        lax.fori_loop(lons // 2, lons, step, 0)
        send_on(g, False)

    def first_part(k, carry):
        send_part(0, k)
        return carry

    lax.fori_loop(0, lons, first_part, 0)

    loads = [
        pltpu.make_async_copy(source, target, weight_sem.at[i])
        for i, (source, target) in enumerate(
            (
                (w_key, key_v),
                (w_value, value_v),
                (w_merge, merge_v),
                (w_qkv, qkv_v),
                (w_out, out_v),
                (w_up, up_v),
                (w_down, down_v),
                (surf, latent.at[0, pl.ds(0, ROWS), pl.ds(0, COLS), :]),
            )
        )
    ]
    for load in loads:
        load.start()
    result[...] = jnp.zeros_like(result)
    latent[:, :, COLS : COLS + GRP, :] = jnp.zeros((LATENT, ROWS + HALO, GRP, D), BF16)
    embed_v[...] = embed_ref[...].astype(F32)

    new = lax.broadcasted_iota(jnp.int32, (D, D), 1)
    old = lax.broadcasted_iota(jnp.int32, (D, D), 0)
    loads[1].wait()
    value_p[...] = dot(
        value_v[...], jnp.where(old == (new % HEADS) * HEAD + new // HEADS, 1.0, 0.0).astype(BF16)
    ).astype(BF16)
    loads[2].wait()
    merge_p[...] = dot(
        jnp.where(new == (old % HEADS) * HEAD + old // HEADS, 1.0, 0.0).astype(BF16), merge_v[...]
    ).astype(BF16)
    loads[0].wait()
    head_of = lax.broadcasted_iota(jnp.int32, (LANES, D), 1) // HEAD
    row_head = lax.broadcasted_iota(jnp.int32, (LANES, D), 0) % HEADS
    for a in range(ATMOS):
        picked = jnp.where(head_of == row_head, queries_ref[a : a + 1, :].astype(F32), 0.0).astype(BF16)
        folded = lax.dot_general(
            picked, key_v[...], (((1,), (1,)), ((), ())), preferred_element_type=F32
        )
        folded = folded.T * (LOG2E / math.sqrt(HEAD))
        high = folded.astype(BF16)
        fold_v[:, a * LANES : (a + 1) * LANES] = high
        fold_v[:, (ATMOS + a) * LANES : (ATMOS + a + 1) * LANES] = (folded - high.astype(F32)).astype(BF16)

    def aggregate(g, h):
        def one_level(j, carry):
            landed = recv.at[g, h, j]
            pltpu.make_async_copy(landed, landed, recv_sem.at[g, h, j]).wait()
            row = embed_v[pl.ds(order_ref[j], 1), :]
            x = landed[...].reshape(PATCHES, D).astype(F32) + row
            normed_v[pl.ds(pl.multiple_of(j * PATCHES, PATCHES), PATCHES), :] = norm(x, kv_gain_ref[...])
            return carry

        lax.fori_loop(0, lats, one_level, 0)
        values_v[...] = dot(normed_v[...], value_p[...]).astype(BF16)
        scores_v[...] = dot(normed_v[...], fold_v[:, : ATMOS * LANES]) + dot(
            normed_v[...], fold_v[:, ATMOS * LANES :]
        )
        for a in range(ATMOS):
            cut = slice(a * LANES, (a + 1) * LANES)
            level = [scores_v[j * PATCHES : (j + 1) * PATCHES, cut] for j in range(lats)]
            top = functools.reduce(jnp.maximum, level)
            level = [jnp.exp2(s - top) for s in level]
            scale = 1.0 / functools.reduce(jnp.add, level)
            level = [e * scale for e in level]
            for c in range(D // LANES):
                lanes = slice(c * LANES, (c + 1) * LANES)
                mixed = functools.reduce(
                    jnp.add,
                    [
                        level[j] * values_v[j * PATCHES : (j + 1) * PATCHES, lanes].astype(F32)
                        for j in range(lats)
                    ],
                )
                mix_v[a * PATCHES : (a + 1) * PATCHES, lanes] = mixed.astype(BF16)
        merged = dot(mix_v[...], merge_p[...])
        for a in range(ATMOS):
            tokens = merged[a * PATCHES : (a + 1) * PATCHES] + queries_ref[a : a + 1, :].astype(F32)
            latent[
                1 + a, pl.ds(pl.multiple_of(h * WIN_LAT, WIN_LAT), WIN_LAT), g * GRP : (g + 1) * GRP, :
            ] = tokens.astype(BF16).reshape(WIN_LAT, GRP, D)

    def aggregate_group(g):
        lax.fori_loop(0, 2, lambda h, carry: (aggregate(g, h), carry)[1], 0)

    def halo(i, levels, rows, cols, to_row, to_col, lat, lon):
        return pltpu.make_async_remote_copy(
            latent.at[pl.ds(*levels), pl.ds(0, rows), pl.ds(cols, GRP), :],
            latent.at[pl.ds(*levels), pl.ds(to_row, rows), pl.ds(to_col, GRP), :],
            halo_send.at[i],
            halo_recv.at[i],
            device_id=(lat, lon),
            device_id_type=MESH,
        )

    every = (0, LATENT)
    row_halos = [
        halo(0, every, HALO, 0, ROWS, 0, north, lo),
        halo(1, every, HALO, GRP, ROWS, GRP, north, lo),
        halo(2, (0, 2), HALO, 2 * GRP, ROWS, 2 * GRP, north, lo),
        halo(3, (2, 2), HALO, 2 * GRP, ROWS, 2 * GRP, north, lo),
    ]

    def packed(cells):
        levels, rows = cells.shape[:2]
        return cells.astype(F32).reshape(levels, rows // 2, GRP, D).astype(BF16)

    def unpacked(cells):
        levels, pairs = cells.shape[:2]
        return cells.astype(F32).reshape(levels, 2 * pairs, EDGE, D).astype(BF16)

    col_halo = pltpu.make_async_remote_copy(
        ahead_out, ahead_in, halo_send.at[4], halo_recv.at[4], device_id=(la, west), device_id_type=MESH
    )
    corner_halo = pltpu.make_async_remote_copy(
        ahead_out.at[:, pl.ds(0, 2), :, :],
        ahead_corner,
        halo_send.at[5],
        halo_recv.at[5],
        device_id=(north, west),
        device_id_type=MESH,
    )

    last = la == lats - 1

    def attend(pair, rw, b):
        first_row = rw * WIN_LAT + 1
        s, t = shift_ref[b, 0], shift_ref[b, 1]
        levels = pl.ds(2 * b, 2)
        columns = (2 * pair, 2 * pair + 1)
        for w, cw in enumerate(columns):
            place = (s - 1) * 32 + t + OFFSETS[cw]
            cells = latent[levels, pl.ds(first_row, 8), BASES[cw] : BASES[cw] + 32, :]
            at = lax.broadcasted_iota(jnp.int32, (SPAN, 512), 1)
            pick = jnp.where(at == to_cells_ref[...] + place, 1.0, 0.0).astype(BF16)
            x_v[w * SPAN : (w + 1) * SPAN, :] = dot(pick, cells.reshape(512, D))
        normed = norm(x_v[...], attn_gain_ref[...])
        q_v[...] = (dot(normed, qkv_v[:, :D]) * (LOG2E / math.sqrt(HEAD))).astype(BF16)
        k_v[...] = dot(normed, qkv_v[:, D : 2 * D]).astype(BF16)
        v_v[...] = dot(normed, qkv_v[:, 2 * D :]).astype(BF16)
        lane_head = lax.broadcasted_iota(jnp.int32, (SPAN, LANES), 1) // HEAD
        ones = jnp.ones((SPAN, LANES), BF16)
        row_of_q = lax.broadcasted_iota(jnp.int32, (SPAN, SPAN), 0)
        row_of_k = lax.broadcasted_iota(jnp.int32, (SPAN, SPAN), 1)
        row_of_q = (row_of_q // WIN_LON) % WIN_LAT
        row_of_k = (row_of_k // WIN_LON) % WIN_LAT
        start = WIN_LAT - s + jnp.where(jnp.logical_and(last, rw == 1), 0, WIN_LAT)

        def window(w, carry):
            at = pl.ds(pl.multiple_of(w * SPAN, 16), SPAN)
            bias = jnp.where((row_of_q >= start) == (row_of_k >= start), 0.0, -1e30)
            for c in range(D // LANES):
                lanes = slice(c * LANES, (c + 1) * LANES)
                q = q_v[at, lanes]
                k = k_v[at, lanes]
                v = jnp.concatenate([v_v[at, lanes], ones], axis=1)
                mixed = jnp.zeros((SPAN, LANES), F32)
                for h in range(LANES // HEAD):
                    own = lane_head == h
                    s = lax.dot_general(
                        jnp.where(own, q, jnp.zeros_like(q)),
                        k,
                        (((1,), (1,)), ((), ())),
                        preferred_element_type=F32,
                    )
                    s = s + bias
                    p = jnp.exp2(s - jnp.max(s, axis=-1, keepdims=True)).astype(BF16)
                    o = dot(p, v)
                    mixed = jnp.where(own, o[:, :LANES] / o[:, LANES:], mixed)
                attended_v[at, lanes] = mixed.astype(BF16)
            return carry

        lax.fori_loop(0, 2, window, 0)
        first = (x_v[...] + dot(attended_v[...], out_v[...])).astype(BF16).astype(F32)
        normed = norm(first, mlp_gain_ref[...])
        total = first
        for c in range(FF // 512):
            cut = slice(c * 512, (c + 1) * 512)
            hidden = gelu(dot(normed, up_v[:, cut])).astype(BF16)
            total = total + dot(hidden, down_v[cut, :])
        y_v[...] = total.astype(BF16)
        for w, cw in enumerate(columns):
            place = (s - 1) * 32 + t + OFFSETS[cw]
            at = lax.broadcasted_iota(jnp.int32, (512, SPAN), 0)
            put = jnp.where(at == from_cells_ref[0:1, :] + place, 1.0, 0.0).astype(BF16)
            moved = dot(put, y_v[w * SPAN : (w + 1) * SPAN, :]).astype(BF16).reshape(2, 8, 32, D)
            where = (levels, pl.ds(first_row, 8), slice(BASES[cw], BASES[cw] + 32))
            result[where] = result[where] + moved

    def back(i, source, target, lat, lon):
        return pltpu.make_async_remote_copy(
            source, target, back_send.at[i], back_recv.at[i], device_id=(lat, lon), device_id_type=MESH
        )

    def back_south(i, b, columns):
        levels = pl.ds(2 * b, 2)
        return back(
            i,
            result.at[levels, pl.ds(ROWS, HALO), pl.ds(*columns), :],
            from_north.at[levels, :, pl.ds(*columns), :],
            south,
            lo,
        )

    def back_east(i, b, pairs):
        where = (pl.ds(2 * b, 2), pl.ds(*pairs))
        return back(i, back_out.at[where], from_west.at[where], la, east)

    def back_corner(i, b):
        levels = pl.ds(2 * b, 2)
        return back(i, back_out.at[levels, pl.ds(ROWS // 2, 2)], from_corner.at[levels], south, east)

    def back_pack(b, first, count):
        levels = slice(2 * b, 2 * b + 2)
        back_out[levels, first : first + count] = packed(
            result[levels, 2 * first : 2 * (first + count), COLS : COLS + EDGE, :]
        )

    first_backs = [back_south(b, b, (0, GRP)) for b in range(2)]
    souths = [back_south(2 + b, b, (GRP, COLS - GRP)) for b in range(2)]
    corners = [back_corner(4 + b, b) for b in range(2)]
    uppers = [back_east(6, 0, (0, 3)), back_east(7, 1, (0, 5))]
    lowers = [back_east(8, 0, (3, 3)), back_east(9, 1, (5, 1))]

    next_group(0)
    aggregate_group(0)
    loads[7].wait()
    ahead_out[...] = packed(latent[:, 0:ROWS, 0:EDGE, :])
    row_halos[0].start()
    corner_halo.start()
    col_halo.start()
    next_group(1)
    aggregate_group(1)
    row_halos[1].start()
    for i in range(3, 7):
        loads[i].wait()

    def first_pair(i, carry):
        @pl.when(i == 1)
        def _():
            send_on(2, True)

        @pl.when(i == 2)
        def _():
            send_on(2, False)
            row_halos[0].wait_recv()
            row_halos[1].wait_recv()

        attend(0, i // 2, lax.rem(i, 2))
        return carry

    lax.fori_loop(0, 4, first_pair, 0)
    for copy in first_backs:
        copy.start()
    aggregate_group(2)
    row_halos[2].start()
    row_halos[3].start()
    col_halo.wait_recv()
    latent[:, 0:ROWS, COLS : COLS + EDGE, :] = unpacked(ahead_in[...])
    corner_halo.wait_recv()
    latent[:, ROWS : ROWS + HALO, COLS : COLS + EDGE, :] = unpacked(ahead_corner[...])[:, :HALO]

    def second_pair(i, carry):
        b = i // 2
        rw = lax.rem(i + b, 2)

        @pl.when(i == 1)
        def _():
            row_halos[2].wait_recv()

        @pl.when(i == 2)
        def _():
            row_halos[3].wait_recv()

        attend(1, rw, b)

        @pl.when(i == 0)
        def _():
            back_pack(0, 0, 3)
            uppers[0].start()

        @pl.when(i == 1)
        def _():
            souths[0].start()
            back_pack(0, 3, 5)
            corners[0].start()
            lowers[0].start()

        @pl.when(i == 2)
        def _():
            souths[1].start()
            back_pack(1, 5, 3)
            corners[1].start()
            lowers[1].start()

        @pl.when(i == 3)
        def _():
            back_pack(1, 0, 5)
            uppers[1].start()

        return carry

    lax.fori_loop(0, 4, second_pair, 0)
    def finished(b):
        levels = pl.ds(2 * b, 2)
        return pltpu.make_async_copy(
            result.at[levels, pl.ds(0, ROWS), pl.ds(0, COLS), :], out.at[levels], out_sem.at[b]
        )

    for b in range(2):
        levels = slice(2 * b, 2 * b + 2)
        for copies in (first_backs, souths, corners, lowers, uppers):
            copies[b].wait_recv()
        result[levels, 0:HALO, 0:COLS, :] = result[levels, 0:HALO, 0:COLS, :] + from_north[levels]
        result[levels, 0:ROWS, 0:EDGE, :] = result[levels, 0:ROWS, 0:EDGE, :] + unpacked(from_west[levels])
        result[levels, 0:HALO, 0:EDGE, :] = (
            result[levels, 0:HALO, 0:EDGE, :] + unpacked(from_corner[levels])[:, :HALO]
        )
        finished(b).start()
    for copies in (first_backs, souths, corners, lowers, uppers):
        for copy in copies:
            copy.wait_send()
    for copy in row_halos + [col_halo, corner_halo]:
        copy.wait_send()

    def sent(k, carry):
        sent_part(GROUPS - 1, k)
        return carry

    lax.fori_loop(0, lons, sent, 0)

    @pl.when(outer)
    def _():
        def step(i, carry):
            relay_copy(i // lats, lax.rem(i, 2), lax.rem(i // 2, half_lats)).wait_send()
            return carry

        lax.fori_loop(0, GROUPS * lats, step, 0)

    for b in range(2):
        finished(b).wait()


def shards(
    lats,
    lons,
    level_slabs,
    surf_tokens,
    level_order,
    level_embed,
    kv_gain,
    latent_queries,
    w_key,
    w_value,
    w_merge,
    attn_gain,
    w_qkv,
    w_out,
    mlp_gain,
    w_up,
    w_down,
    window_shift,
):
    token = np.arange(SPAN)
    cell = (token // 72) * 256 + (token % 72) // 12 * 32 + token % 12
    to_cells = jnp.asarray(cell[:, None], jnp.int32)
    from_cells = jnp.asarray(np.broadcast_to(cell[None, :], (8, SPAN)), jnp.int32)
    smem = pl.BlockSpec(memory_space=pltpu.SMEM)
    vmem = pl.BlockSpec(memory_space=pltpu.VMEM)
    hbm = pl.BlockSpec(memory_space=pl.ANY)
    tokens = lats * PATCHES
    return pl.pallas_call(
        functools.partial(kernel, lats, lons),
        out_shape=jax.ShapeDtypeStruct((LATENT, ROWS, COLS, D), BF16),
        in_specs=[smem] * 2 + [hbm] * 2 + [vmem] * 7 + [hbm] * 7,
        out_specs=hbm,
        scratch_shapes=[
            pltpu.VMEM((GROUPS, 2, lats, WIN_LAT, GRP, D), BF16),
            pltpu.VMEM((GROUPS, 2, lats // 2, WIN_LAT, GRP, D), BF16),
            pltpu.VMEM((LATENT, ROWS + HALO, COLS + GRP, D), BF16),
            pltpu.VMEM((LATENT, ROWS + HALO + 1, COLS + GRP, D), BF16),
            pltpu.VMEM((LATENT, HALO, COLS, D), BF16),
            pltpu.VMEM((LATENT, ROWS // 2, GRP, D), BF16),
            pltpu.VMEM((LATENT, 2, GRP, D), BF16),
            pltpu.VMEM((LATENT, ROWS // 2, GRP, D), BF16),
            pltpu.VMEM((LATENT, ROWS // 2, GRP, D), BF16),
            pltpu.VMEM((LATENT, 2, GRP, D), BF16),
            pltpu.VMEM((LATENT, ROWS // 2 + 2, GRP, D), BF16),
            pltpu.VMEM((D, D), BF16),
            pltpu.VMEM((D, D), BF16),
            pltpu.VMEM((D, D), BF16),
            pltpu.VMEM((D, 3 * D), BF16),
            pltpu.VMEM((D, D), BF16),
            pltpu.VMEM((D, FF), BF16),
            pltpu.VMEM((FF, D), BF16),
            pltpu.VMEM((lats, D), F32),
            pltpu.VMEM((D, 2 * ATMOS * LANES), BF16),
            pltpu.VMEM((D, D), BF16),
            pltpu.VMEM((D, D), BF16),
            pltpu.VMEM((tokens, D), BF16),
            pltpu.VMEM((tokens, D), BF16),
            pltpu.VMEM((tokens, ATMOS * LANES), F32),
            pltpu.VMEM((ATMOS * PATCHES, D), BF16),
            pltpu.VMEM((BATCH, D), F32),
            pltpu.VMEM((BATCH, D), BF16),
            pltpu.VMEM((BATCH, D), BF16),
            pltpu.VMEM((BATCH, D), BF16),
            pltpu.VMEM((BATCH, D), BF16),
            pltpu.VMEM((BATCH, D), BF16),
            pltpu.SemaphoreType.DMA((GROUPS, lons)),
            pltpu.SemaphoreType.DMA((GROUPS, 2, lats)),
            pltpu.SemaphoreType.DMA((GROUPS, 2, lats // 2)),
            pltpu.SemaphoreType.DMA((GROUPS, 2, lats // 2)),
            pltpu.SemaphoreType.DMA((8,)),
            pltpu.SemaphoreType.DMA((6,)),
            pltpu.SemaphoreType.DMA((6,)),
            pltpu.SemaphoreType.DMA((10,)),
            pltpu.SemaphoreType.DMA((10,)),
            pltpu.SemaphoreType.DMA((2,)),
        ],
        compiler_params=pltpu.CompilerParams(
            collective_id=0, has_side_effects=True, vmem_limit_bytes=56 * 1024 * 1024
        ),
        name="encoder",
    )(
        level_order,
        window_shift,
        level_slabs,
        surf_tokens,
        level_embed,
        kv_gain.reshape(1, D),
        latent_queries,
        attn_gain.reshape(1, D),
        mlp_gain.reshape(1, D),
        to_cells,
        from_cells,
        w_key,
        w_value,
        w_merge,
        w_qkv,
        w_out,
        w_up,
        w_down,
    )


def solution(mesh):
    in_specs = (P("lat", "lon", None, None), P("lat", "lon", None)) + (P(),) * 14
    return jax.shard_map(
        functools.partial(shards, mesh.shape["lat"], mesh.shape["lon"]),
        mesh=mesh,
        in_specs=in_specs,
        out_specs=P(None, "lat", "lon", None),
        check_vma=False,
    )
```

```python
import functools
import math

import jax
import jax.numpy as jnp
import numpy as np
from jax import lax
from jax.experimental import pallas as pl
from jax.experimental.pallas import tpu as pltpu
from jax.sharding import PartitionSpec as P

D = 512
HEADS = 16
HEAD = D // HEADS
FF = 2048
ATMOS = 3
LATENT = 4
WIN_LAT = 6
WIN_LON = 12
SPAN = 2 * WIN_LAT * WIN_LON
ROWS = 12
COLS = 48
GRP = 16
GROUPS = COLS // GRP
HALO = 3
SUB = WIN_LAT // 2
STEPS = 2 * GROUPS
AHEAD = 2
EDGE = 8
PATCHES = 2 * (WIN_LAT // 2) * GRP
BATCH = 4 * SPAN
LANES = 128
LOG2E = math.log2(math.e)
MESH = pl.DeviceIdType.MESH
F32 = jnp.float32
BF16 = jnp.bfloat16
BASES = (0, 0, 16, 32)
OFFSETS = (0, 12, 8, 4)


def dot(a, b):
    return jnp.dot(a, b, preferred_element_type=F32)


def norm(x, gain):
    mean = jnp.mean(x, axis=-1, keepdims=True)
    centred = x - mean
    variance = jnp.mean(centred * centred, axis=-1, keepdims=True)
    return (centred * lax.rsqrt(variance + 1e-05) * gain).astype(BF16)


def gelu(x):
    c = math.sqrt(2.0 / math.pi)
    return 0.5 * x * (1.0 + jnp.tanh(x * (c + (c * 0.044715) * (x * x))))


def kernel(
    lats,
    lons,
    order_ref,
    shift_ref,
    slabs,
    surf,
    embed_ref,
    kv_gain_ref,
    queries_ref,
    attn_gain_ref,
    mlp_gain_ref,
    to_cells_ref,
    from_cells_ref,
    w_key,
    w_value,
    w_merge,
    w_qkv,
    w_out,
    w_up,
    w_down,
    out,
    recv,
    relay,
    latent,
    result,
    from_north,
    from_west,
    from_corner,
    ahead_out,
    ahead_in,
    ahead_corner,
    back_out,
    key_v,
    value_v,
    merge_v,
    qkv_v,
    out_v,
    up_v,
    down_v,
    embed_v,
    fold_v,
    value_p,
    merge_p,
    normed_v,
    values_v,
    scores_v,
    mix_v,
    x_v,
    q_v,
    k_v,
    v_v,
    attended_v,
    y_v,
    send_sem,
    recv_sem,
    relay_send,
    relay_recv,
    weight_sem,
    halo_send,
    halo_recv,
    back_send,
    back_recv,
    out_sem,
):
    la = lax.axis_index("lat")
    lo = lax.axis_index("lon")
    north = lax.rem(la + lats - 1, lats)
    south = lax.rem(la + 1, lats)
    west = lax.rem(lo + lons - 1, lons)
    east = lax.rem(lo + 1, lons)
    half = lax.rem(lo, 2)
    dest_lat = lo // 2
    has_self = dest_lat == la
    half_lats, half_lons = lats // 2, lons // 2
    z_lo, z_hi = la // half_lats, lo // half_lons
    outer = z_lo == z_hi
    across = lax.rem(la + half_lats, lats)

    def is_self(lat, lon):
        return jnp.logical_and(lat == la, lon == lo)

    barrier = pltpu.get_barrier_semaphore()

    def greet(lat, lon):
        pl.semaphore_signal(barrier, inc=1, device_id=(lat, lon), device_id_type=MESH)

    for lat in range(lats):
        for r in range(2):
            lon = 2 * la + r
            by_relay = jnp.logical_and(jnp.logical_not(outer), lat // half_lats == z_lo)

            @pl.when(jnp.logical_not(jnp.logical_or(is_self(lat, lon), by_relay)))
            def _():
                greet(lat, lon)

    @pl.when(jnp.logical_not(outer))
    def _():
        greet(across, lo)

    @pl.when(outer)
    def _():
        for y in range(half_lats):
            for r in range(2):
                greet((1 - z_lo) * half_lats + y, 2 * across + r)

    for lat, lon in ((south, lo), (la, east), (south, east), (north, lo), (la, west), (north, west)):
        greet(lat, lon)
    pl.semaphore_wait(barrier, 6 + 2 * lats + jnp.where(outer, 1, 0) - jnp.where(has_self, 1, 0))

    def part_to(k):
        x = lax.rem(lax.rem(lo, half_lons) // 2 + k, half_lats)
        core = lax.rem(half + k // half_lons, 2)
        return lax.rem(z_hi + 1 + k // half_lats, 2) * half_lons + 2 * x + core

    def relayed(lon):
        return jnp.logical_and(outer, lon // half_lons != z_hi)

    def part_copies(n, k):
        lon = part_to(k)
        source = slabs.at[
            0,
            pl.ds(lax.rem(n, 2) * SUB, SUB),
            pl.ds(pl.multiple_of(lon * COLS + n // 2 * GRP, GRP), GRP),
            :,
        ]
        target = recv.at[n, la, half]
        y = lax.rem(la, half_lats)
        return (
            pltpu.make_async_copy(source, target, recv_sem.at[n, la, half]),
            pltpu.make_async_remote_copy(
                source,
                target,
                send_sem.at[n, k],
                recv_sem.at[n, la, half],
                device_id=(dest_lat, lon),
                device_id_type=MESH,
            ),
            pltpu.make_async_remote_copy(
                source,
                relay.at[n, y, half],
                send_sem.at[n, k],
                relay_recv.at[n, y, half],
                device_id=(lax.rem(dest_lat + half_lats, lats), lon),
                device_id_type=MESH,
            ),
        )

    def send_part(n, k):
        lon = part_to(k)
        own = is_self(dest_lat, lon)

        @pl.when(own)
        def _():
            part_copies(n, k)[0].start()

        @pl.when(relayed(lon))
        def _():
            part_copies(n, k)[2].start()

        @pl.when(jnp.logical_not(jnp.logical_or(own, relayed(lon))))
        def _():
            part_copies(n, k)[1].start()

    def sent_part(n, k):
        @pl.when(jnp.logical_not(is_self(dest_lat, part_to(k))))
        def _():
            part_copies(n, k)[1].wait_send()

    def relay_copy(n, y, h):
        level = (1 - z_lo) * half_lats + y
        return pltpu.make_async_remote_copy(
            relay.at[n, y, h],
            recv.at[n, level, h],
            relay_send.at[n, y, h],
            recv_sem.at[n, level, h],
            device_id=(across, lo),
            device_id_type=MESH,
        )

    def send_on(n, first):
        @pl.when(outer)
        def _():
            h = half if first else 1 - half

            def step(y, carry):
                landed = relay.at[n, y, h]
                pltpu.make_async_copy(landed, landed, relay_recv.at[n, y, h]).wait()
                relay_copy(n, y, h).start()
                return carry

            lax.fori_loop(0, half_lats, step, 0)

    def next_step(n):
        def step(k, carry):
            sent_part(n, k)
            send_part(n + AHEAD, k)
            return carry

        lax.fori_loop(0, lons // 2, step, 0)
        send_on(n, True)
        lax.fori_loop(lons // 2, lons, step, 0)
        send_on(n, False)

    def first_part(i, carry):
        send_part(i // lons, lax.rem(i, lons))
        return carry

    lax.fori_loop(0, AHEAD * lons, first_part, 0)

    loads = [
        pltpu.make_async_copy(source, target, weight_sem.at[i])
        for i, (source, target) in enumerate(
            (
                (w_key, key_v),
                (w_value, value_v),
                (w_merge, merge_v),
                (w_qkv, qkv_v),
                (w_out, out_v),
                (w_up, up_v),
                (w_down, down_v),
                (surf, latent.at[0, pl.ds(0, ROWS), pl.ds(0, COLS), :]),
            )
        )
    ]
    for load in loads:
        load.start()
    result[...] = jnp.zeros_like(result)
    latent[:, :, COLS : COLS + GRP, :] = jnp.zeros((LATENT, ROWS + HALO, GRP, D), BF16)
    embed_v[...] = embed_ref[...].astype(F32)

    new = lax.broadcasted_iota(jnp.int32, (D, D), 1)
    old = lax.broadcasted_iota(jnp.int32, (D, D), 0)
    loads[1].wait()
    value_p[...] = dot(
        value_v[...], jnp.where(old == (new % HEADS) * HEAD + new // HEADS, 1.0, 0.0).astype(BF16)
    ).astype(BF16)
    loads[2].wait()
    merge_p[...] = dot(
        jnp.where(new == (old % HEADS) * HEAD + old // HEADS, 1.0, 0.0).astype(BF16), merge_v[...]
    ).astype(BF16)
    loads[0].wait()
    head_of = lax.broadcasted_iota(jnp.int32, (LANES, D), 1) // HEAD
    row_head = lax.broadcasted_iota(jnp.int32, (LANES, D), 0) % HEADS
    for a in range(ATMOS):
        picked = jnp.where(head_of == row_head, queries_ref[a : a + 1, :].astype(F32), 0.0).astype(BF16)
        folded = lax.dot_general(
            picked, key_v[...], (((1,), (1,)), ((), ())), preferred_element_type=F32
        )
        folded = folded.T * (LOG2E / math.sqrt(HEAD))
        fold_v[:, a * LANES : (a + 1) * LANES] = folded.astype(BF16)

    def aggregate(n):
        def landing(i, carry):
            j, h = i // 2, lax.rem(i, 2)
            landed = recv.at[n, j, h]
            pltpu.make_async_copy(landed, landed, recv_sem.at[n, j, h]).wait()
            return carry

        lax.fori_loop(0, 2 * lats, landing, 0)
        for j in range(lats):
            row = embed_v[pl.ds(order_ref[j], 1), :]
            x = recv[n, j].reshape(PATCHES, D).astype(F32) + row
            normed_v[j * PATCHES : (j + 1) * PATCHES, :] = norm(x, kv_gain_ref[...])
        values_v[...] = dot(normed_v[...], value_p[...]).astype(BF16)
        scores_v[...] = dot(normed_v[...], fold_v[...])
        for a in range(ATMOS):
            cut = slice(a * LANES, (a + 1) * LANES)
            level = [scores_v[j * PATCHES : (j + 1) * PATCHES, cut] for j in range(lats)]
            top = functools.reduce(jnp.maximum, level)
            level = [jnp.exp2(s - top) for s in level]
            scale = 1.0 / functools.reduce(jnp.add, level)
            level = [e * scale for e in level]
            for c in range(D // LANES):
                lanes = slice(c * LANES, (c + 1) * LANES)
                mixed = functools.reduce(
                    jnp.add,
                    [
                        level[j] * values_v[j * PATCHES : (j + 1) * PATCHES, lanes].astype(F32)
                        for j in range(lats)
                    ],
                )
                mix_v[a * PATCHES : (a + 1) * PATCHES, lanes] = mixed.astype(BF16)
        merged = dot(mix_v[...], merge_p[...])
        for a in range(ATMOS):
            tokens = merged[a * PATCHES : (a + 1) * PATCHES] + queries_ref[a : a + 1, :].astype(F32)
            tokens = tokens.astype(BF16).reshape(2, SUB, GRP, D)
            for h in range(2):
                first = h * WIN_LAT + n % 2 * SUB
                latent[1 + a, first : first + SUB, n // 2 * GRP : (n // 2 + 1) * GRP, :] = tokens[h]

    def halo(i, levels, rows, cols, to_row, to_col, lat, lon):
        return pltpu.make_async_remote_copy(
            latent.at[pl.ds(*levels), pl.ds(0, rows), pl.ds(cols, GRP), :],
            latent.at[pl.ds(*levels), pl.ds(to_row, rows), pl.ds(to_col, GRP), :],
            halo_send.at[i],
            halo_recv.at[i],
            device_id=(lat, lon),
            device_id_type=MESH,
        )

    every = (0, LATENT)
    row_halos = [halo(g, every, HALO, g * GRP, ROWS, g * GRP, north, lo) for g in range(GROUPS)]

    def packed(cells):
        levels, rows = cells.shape[:2]
        return cells.astype(F32).reshape(levels, rows // 2, GRP, D).astype(BF16)

    def unpacked(cells):
        levels, pairs = cells.shape[:2]
        return cells.astype(F32).reshape(levels, 2 * pairs, EDGE, D).astype(BF16)

    col_halo = pltpu.make_async_remote_copy(
        ahead_out, ahead_in, halo_send.at[4], halo_recv.at[4], device_id=(la, west), device_id_type=MESH
    )
    corner_halo = pltpu.make_async_remote_copy(
        ahead_out.at[:, pl.ds(0, 2), :, :],
        ahead_corner,
        halo_send.at[5],
        halo_recv.at[5],
        device_id=(north, west),
        device_id_type=MESH,
    )

    last = la == lats - 1

    def attend(rw, windows, halfway=None):
        first_row = rw * WIN_LAT + 1
        rows = slice(0, len(windows) * SPAN)

        def place(b, cw):
            return (shift_ref[b, 0] - 1) * 32 + shift_ref[b, 1] + OFFSETS[cw]

        for w, (b, cw) in enumerate(windows):
            cells = latent[pl.ds(2 * b, 2), pl.ds(first_row, 8), BASES[cw] : BASES[cw] + 32, :]
            at = lax.broadcasted_iota(jnp.int32, (SPAN, 512), 1)
            pick = jnp.where(at == to_cells_ref[...] + place(b, cw), 1.0, 0.0).astype(BF16)
            x_v[w * SPAN : (w + 1) * SPAN, :] = dot(pick, cells.reshape(512, D))
        normed = norm(x_v[rows, :], attn_gain_ref[...])
        q_v[rows, :] = (dot(normed, qkv_v[:, :D]) * (LOG2E / math.sqrt(HEAD))).astype(BF16)
        k_v[rows, :] = dot(normed, qkv_v[:, D : 2 * D]).astype(BF16)
        v_v[rows, :] = dot(normed, qkv_v[:, 2 * D :]).astype(BF16)
        lane_head = lax.broadcasted_iota(jnp.int32, (SPAN, LANES), 1) // HEAD
        ones = jnp.ones((SPAN, LANES), BF16)
        row_of_q = lax.broadcasted_iota(jnp.int32, (SPAN, SPAN), 0)
        row_of_k = lax.broadcasted_iota(jnp.int32, (SPAN, SPAN), 1)
        row_of_q = (row_of_q // WIN_LON) % WIN_LAT
        row_of_k = (row_of_k // WIN_LON) % WIN_LAT
        beyond = jnp.where(jnp.logical_and(last, rw == 1), 0, WIN_LAT)

        heads = LANES // HEAD
        own = [lane_head == h for h in range(heads)]

        def window(w, bias):
            at = slice(w * SPAN, (w + 1) * SPAN)
            for c in range(D // LANES):
                lanes = slice(c * LANES, (c + 1) * LANES)
                q = q_v[at, lanes]
                q = jnp.concatenate([jnp.where(own[h], q, jnp.zeros_like(q)) for h in range(heads)], axis=0)
                v = jnp.concatenate([v_v[at, lanes], ones], axis=1)
                s = lax.dot_general(
                    q, k_v[at, lanes], (((1,), (1,)), ((), ())), preferred_element_type=F32
                )
                s = s + bias
                p = jnp.exp2(s - jnp.max(s, axis=-1, keepdims=True)).astype(BF16)
                o = dot(p, v)
                o = o[:, :LANES] * pl.reciprocal(o[:, LANES:], approx=True)
                mixed = o[:SPAN]
                for h in range(1, heads):
                    mixed = jnp.where(own[h], o[h * SPAN : (h + 1) * SPAN], mixed)
                attended_v[at, lanes] = mixed.astype(BF16)

        for b in range(2):
            start = WIN_LAT - shift_ref[b, 0] + beyond
            bias = jnp.where((row_of_q >= start) == (row_of_k >= start), 0.0, -1e30)
            bias = jnp.concatenate([bias] * heads, axis=0)
            for w in range(len(windows)):
                if windows[w][0] == b:
                    window(w, bias)
        if halfway is not None:
            halfway()
        first = (x_v[rows, :] + dot(attended_v[rows, :], out_v[...])).astype(BF16).astype(F32)
        normed = norm(first, mlp_gain_ref[...])
        total = first
        for c in range(FF // 512):
            cut = slice(c * 512, (c + 1) * 512)
            hidden = gelu(dot(normed, up_v[:, cut])).astype(BF16)
            total = total + dot(hidden, down_v[cut, :])
        y_v[rows, :] = total.astype(BF16)
        for w, (b, cw) in enumerate(windows):
            at = lax.broadcasted_iota(jnp.int32, (512, SPAN), 0)
            put = jnp.where(at == from_cells_ref[0:1, :] + place(b, cw), 1.0, 0.0).astype(BF16)
            moved = dot(put, y_v[w * SPAN : (w + 1) * SPAN, :]).astype(BF16).reshape(2, 8, 32, D)
            where = (pl.ds(2 * b, 2), pl.ds(first_row, 8), slice(BASES[cw], BASES[cw] + 32))
            result[where] = result[where] + moved

    def back(i, source, target, lat, lon):
        return pltpu.make_async_remote_copy(
            source, target, back_send.at[i], back_recv.at[i], device_id=(lat, lon), device_id_type=MESH
        )

    def back_south(i, columns):
        return back(
            i,
            result.at[:, pl.ds(ROWS, HALO), pl.ds(*columns), :],
            from_north.at[:, :, pl.ds(*columns), :],
            south,
            lo,
        )

    def back_east(i, pairs):
        return back(i, back_out.at[:, pl.ds(*pairs)], from_west.at[:, pl.ds(*pairs)], la, east)

    def back_pack(first, count):
        back_out[:, first : first + count] = packed(
            result[:, 2 * first : 2 * (first + count), COLS : COLS + EDGE, :]
        )

    backs = (
        back_south(0, (0, GRP)),
        back_south(1, (GRP, COLS - GRP)),
        back(2, back_out.at[:, pl.ds(ROWS // 2, 2)], from_corner, south, east),
        back_east(3, (5, 1)),
        back_east(4, (0, 5)),
    )

    next_step(0)
    aggregate(0)
    loads[7].wait()
    row_halos[0].start()
    next_step(1)
    aggregate(1)
    ahead_out[...] = packed(latent[:, 0:ROWS, 0:EDGE, :])
    corner_halo.start()
    col_halo.start()
    next_step(2)
    aggregate(2)
    row_halos[1].start()
    next_step(3)
    aggregate(3)
    for i in range(3, 7):
        loads[i].wait()

    def first_pair(rw, carry):
        @pl.when(rw == 0)
        def _():
            send_on(4, True)

        @pl.when(rw == 1)
        def _():
            send_on(5, True)
            row_halos[0].wait_recv()
            row_halos[1].wait_recv()

        def halfway():
            @pl.when(rw == 0)
            def _():
                send_on(4, False)

            @pl.when(rw == 1)
            def _():
                send_on(5, False)

        attend(rw, [(b, cw) for b in range(2) for cw in (0, 1)], halfway)
        return carry

    lax.fori_loop(0, 2, first_pair, 0)
    backs[0].start()
    aggregate(4)
    row_halos[2].start()
    col_halo.wait_recv()
    latent[:, 0:ROWS, COLS : COLS + EDGE, :] = unpacked(ahead_in[...])
    corner_halo.wait_recv()
    latent[:, ROWS : ROWS + HALO, COLS : COLS + EDGE, :] = unpacked(ahead_corner[...])[:, :HALO]
    aggregate(5)
    row_halos[2].wait_recv()
    attend(1, [(b, cw) for b in range(2) for cw in (2, 3)])
    backs[1].start()
    back_pack(5, 3)
    backs[2].start()
    backs[3].start()
    attend(0, [(b, 3) for b in range(2)])
    back_pack(0, 5)
    backs[4].start()
    attend(0, [(b, 2) for b in range(2)])

    def finished(b):
        levels = pl.ds(2 * b, 2)
        return pltpu.make_async_copy(
            result.at[levels, pl.ds(0, ROWS), pl.ds(0, COLS), :], out.at[levels], out_sem.at[b]
        )

    for copy in backs:
        copy.wait_recv()
    for b in range(2):
        levels = slice(2 * b, 2 * b + 2)
        result[levels, 0:HALO, 0:COLS, :] = result[levels, 0:HALO, 0:COLS, :] + from_north[levels]
        result[levels, 0:ROWS, 0:EDGE, :] = result[levels, 0:ROWS, 0:EDGE, :] + unpacked(from_west[levels])
        result[levels, 0:HALO, 0:EDGE, :] = (
            result[levels, 0:HALO, 0:EDGE, :] + unpacked(from_corner[levels])[:, :HALO]
        )
        finished(b).start()
    for copy in backs:
        copy.wait_send()
    for copy in row_halos + [col_halo, corner_halo]:
        copy.wait_send()

    def sent(i, carry):
        sent_part(STEPS - AHEAD + i // lons, lax.rem(i, lons))
        return carry

    lax.fori_loop(0, AHEAD * lons, sent, 0)

    @pl.when(outer)
    def _():
        def step(i, carry):
            relay_copy(i // lats, lax.rem(i, lats) // 2, lax.rem(i, 2)).wait_send()
            return carry

        lax.fori_loop(0, STEPS * lats, step, 0)

    for b in range(2):
        finished(b).wait()


def shards(
    lats,
    lons,
    level_slabs,
    surf_tokens,
    level_order,
    level_embed,
    kv_gain,
    latent_queries,
    w_key,
    w_value,
    w_merge,
    attn_gain,
    w_qkv,
    w_out,
    mlp_gain,
    w_up,
    w_down,
    window_shift,
):
    token = np.arange(SPAN)
    cell = (token // 72) * 256 + (token % 72) // 12 * 32 + token % 12
    to_cells = jnp.asarray(cell[:, None], jnp.int32)
    from_cells = jnp.asarray(np.broadcast_to(cell[None, :], (8, SPAN)), jnp.int32)
    smem = pl.BlockSpec(memory_space=pltpu.SMEM)
    vmem = pl.BlockSpec(memory_space=pltpu.VMEM)
    hbm = pl.BlockSpec(memory_space=pl.ANY)
    tokens = lats * PATCHES
    return pl.pallas_call(
        functools.partial(kernel, lats, lons),
        out_shape=jax.ShapeDtypeStruct((LATENT, ROWS, COLS, D), BF16),
        in_specs=[smem] * 2 + [hbm] * 2 + [vmem] * 7 + [hbm] * 7,
        out_specs=hbm,
        scratch_shapes=[
            pltpu.VMEM((STEPS, lats, 2, SUB, GRP, D), BF16),
            pltpu.VMEM((STEPS, lats // 2, 2, SUB, GRP, D), BF16),
            pltpu.VMEM((LATENT, ROWS + HALO, COLS + GRP, D), BF16),
            pltpu.VMEM((LATENT, ROWS + HALO + 1, COLS + GRP, D), BF16),
            pltpu.VMEM((LATENT, HALO, COLS, D), BF16),
            pltpu.VMEM((LATENT, ROWS // 2, GRP, D), BF16),
            pltpu.VMEM((LATENT, 2, GRP, D), BF16),
            pltpu.VMEM((LATENT, ROWS // 2, GRP, D), BF16),
            pltpu.VMEM((LATENT, ROWS // 2, GRP, D), BF16),
            pltpu.VMEM((LATENT, 2, GRP, D), BF16),
            pltpu.VMEM((LATENT, ROWS // 2 + 2, GRP, D), BF16),
            pltpu.VMEM((D, D), BF16),
            pltpu.VMEM((D, D), BF16),
            pltpu.VMEM((D, D), BF16),
            pltpu.VMEM((D, 3 * D), BF16),
            pltpu.VMEM((D, D), BF16),
            pltpu.VMEM((D, FF), BF16),
            pltpu.VMEM((FF, D), BF16),
            pltpu.VMEM((lats, D), F32),
            pltpu.VMEM((D, ATMOS * LANES), BF16),
            pltpu.VMEM((D, D), BF16),
            pltpu.VMEM((D, D), BF16),
            pltpu.VMEM((tokens, D), BF16),
            pltpu.VMEM((tokens, D), BF16),
            pltpu.VMEM((tokens, ATMOS * LANES), F32),
            pltpu.VMEM((ATMOS * PATCHES, D), BF16),
            pltpu.VMEM((BATCH, D), F32),
            pltpu.VMEM((BATCH, D), BF16),
            pltpu.VMEM((BATCH, D), BF16),
            pltpu.VMEM((BATCH, D), BF16),
            pltpu.VMEM((BATCH, D), BF16),
            pltpu.VMEM((BATCH, D), BF16),
            pltpu.SemaphoreType.DMA((STEPS, lons)),
            pltpu.SemaphoreType.DMA((STEPS, lats, 2)),
            pltpu.SemaphoreType.DMA((STEPS, lats // 2, 2)),
            pltpu.SemaphoreType.DMA((STEPS, lats // 2, 2)),
            pltpu.SemaphoreType.DMA((8,)),
            pltpu.SemaphoreType.DMA((6,)),
            pltpu.SemaphoreType.DMA((6,)),
            pltpu.SemaphoreType.DMA((5,)),
            pltpu.SemaphoreType.DMA((5,)),
            pltpu.SemaphoreType.DMA((2,)),
        ],
        compiler_params=pltpu.CompilerParams(
            collective_id=0, has_side_effects=True, vmem_limit_bytes=56 * 1024 * 1024
        ),
        name="encoder",
    )(
        level_order,
        window_shift,
        level_slabs,
        surf_tokens,
        level_embed,
        kv_gain.reshape(1, D),
        latent_queries,
        attn_gain.reshape(1, D),
        mlp_gain.reshape(1, D),
        to_cells,
        from_cells,
        w_key,
        w_value,
        w_merge,
        w_qkv,
        w_out,
        w_up,
        w_down,
    )


def solution(mesh):
    in_specs = (P("lat", "lon", None, None), P("lat", "lon", None)) + (P(),) * 14
    return jax.shard_map(
        functools.partial(shards, mesh.shape["lat"], mesh.shape["lon"]),
        mesh=mesh,
        in_specs=in_specs,
        out_specs=P(None, "lat", "lon", None),
        check_vma=False,
    )
```

```python
import functools
import math

import jax
import jax.numpy as jnp
import numpy as np
from jax import lax
from jax.experimental import pallas as pl
from jax.experimental.pallas import tpu as pltpu
from jax.sharding import PartitionSpec as P

D = 512
HEADS = 16
HEAD = D // HEADS
FF = 2048
ATMOS = 3
LATENT = 4
WIN_LAT = 6
WIN_LON = 12
SPAN = 2 * WIN_LAT * WIN_LON
ROWS = 12
COLS = 48
GRP = 16
GROUPS = COLS // GRP
HALO = 3
SUB = WIN_LAT // 2
STEPS = 2 * GROUPS
AHEAD = 2
EDGE = 8
PATCHES = 2 * (WIN_LAT // 2) * GRP
BATCH = 4 * SPAN
LANES = 128
LOG2E = math.log2(math.e)
MESH = pl.DeviceIdType.MESH
F32 = jnp.float32
BF16 = jnp.bfloat16
BASES = (0, 0, 16, 32)
OFFSETS = (0, 12, 8, 4)


def dot(a, b):
    return jnp.dot(a, b, preferred_element_type=F32)


def norm(x, gain):
    mean = jnp.mean(x, axis=-1, keepdims=True)
    centred = x - mean
    variance = jnp.mean(centred * centred, axis=-1, keepdims=True)
    return (centred * lax.rsqrt(variance + 1e-05) * gain).astype(BF16)


def gelu(x):
    c = math.sqrt(2.0 / math.pi)
    return 0.5 * x * (1.0 + jnp.tanh(x * (c + (c * 0.044715) * (x * x))))


def kernel(
    lats,
    lons,
    order_ref,
    shift_ref,
    slabs,
    surf,
    embed_ref,
    kv_gain_ref,
    queries_ref,
    attn_gain_ref,
    mlp_gain_ref,
    to_cells_ref,
    from_cells_ref,
    w_key,
    w_value,
    w_merge,
    w_qkv,
    w_out,
    w_up,
    w_down,
    out,
    recv,
    relay,
    latent,
    result,
    from_north,
    from_west,
    from_corner,
    ahead_out,
    ahead_in,
    ahead_corner,
    back_out,
    key_v,
    value_v,
    merge_v,
    qkv_v,
    out_v,
    up_v,
    down_v,
    embed_v,
    fold_v,
    value_p,
    merge_p,
    normed_v,
    values_v,
    scores_v,
    mix_v,
    x_v,
    q_v,
    k_v,
    v_v,
    attended_v,
    y_v,
    send_sem,
    recv_sem,
    relay_send,
    relay_recv,
    weight_sem,
    halo_send,
    halo_recv,
    back_send,
    back_recv,
    out_sem,
):
    la = lax.axis_index("lat")
    lo = lax.axis_index("lon")
    north = lax.rem(la + lats - 1, lats)
    south = lax.rem(la + 1, lats)
    west = lax.rem(lo + lons - 1, lons)
    east = lax.rem(lo + 1, lons)
    half = lax.rem(lo, 2)
    dest_lat = lo // 2
    has_self = dest_lat == la
    half_lats, half_lons = lats // 2, lons // 2
    z_lo, z_hi = la // half_lats, lo // half_lons
    outer = z_lo == z_hi
    across = lax.rem(la + half_lats, lats)

    def is_self(lat, lon):
        return jnp.logical_and(lat == la, lon == lo)

    barrier = pltpu.get_barrier_semaphore()

    def greet(lat, lon):
        pl.semaphore_signal(barrier, inc=1, device_id=(lat, lon), device_id_type=MESH)

    for lat in range(lats):
        for r in range(2):
            lon = 2 * la + r
            by_relay = jnp.logical_and(jnp.logical_not(outer), lat // half_lats == z_lo)

            @pl.when(jnp.logical_not(jnp.logical_or(is_self(lat, lon), by_relay)))
            def _():
                greet(lat, lon)

    @pl.when(jnp.logical_not(outer))
    def _():
        greet(across, lo)

    @pl.when(outer)
    def _():
        for y in range(half_lats):
            for r in range(2):
                greet((1 - z_lo) * half_lats + y, 2 * across + r)

    for lat, lon in ((south, lo), (la, east), (south, east), (north, lo), (la, west), (north, west)):
        greet(lat, lon)
    pl.semaphore_wait(barrier, 6 + 2 * lats + jnp.where(outer, 1, 0) - jnp.where(has_self, 1, 0))

    def part_to(k):
        x = lax.rem(lax.rem(lo, half_lons) // 2 + k, half_lats)
        core = lax.rem(half + k // half_lons, 2)
        return lax.rem(z_hi + 1 + k // half_lats, 2) * half_lons + 2 * x + core

    def relayed(lon):
        return jnp.logical_and(outer, lon // half_lons != z_hi)

    def part_copies(n, k):
        lon = part_to(k)
        source = slabs.at[
            0,
            pl.ds(lax.rem(n, 2) * SUB, SUB),
            pl.ds(pl.multiple_of(lon * COLS + n // 2 * GRP, GRP), GRP),
            :,
        ]
        target = recv.at[n, la, half]
        y = lax.rem(la, half_lats)
        return (
            pltpu.make_async_copy(source, target, recv_sem.at[n, la, half]),
            pltpu.make_async_remote_copy(
                source,
                target,
                send_sem.at[n, k],
                recv_sem.at[n, la, half],
                device_id=(dest_lat, lon),
                device_id_type=MESH,
            ),
            pltpu.make_async_remote_copy(
                source,
                relay.at[n, y, half],
                send_sem.at[n, k],
                relay_recv.at[n, y, half],
                device_id=(lax.rem(dest_lat + half_lats, lats), lon),
                device_id_type=MESH,
            ),
        )

    def send_part(n, k):
        lon = part_to(k)
        own = is_self(dest_lat, lon)

        @pl.when(own)
        def _():
            part_copies(n, k)[0].start()

        @pl.when(relayed(lon))
        def _():
            part_copies(n, k)[2].start()

        @pl.when(jnp.logical_not(jnp.logical_or(own, relayed(lon))))
        def _():
            part_copies(n, k)[1].start()

    def sent_part(n, k):
        @pl.when(jnp.logical_not(is_self(dest_lat, part_to(k))))
        def _():
            part_copies(n, k)[1].wait_send()

    def relay_copy(n, y, h):
        level = (1 - z_lo) * half_lats + y
        return pltpu.make_async_remote_copy(
            relay.at[n, y, h],
            recv.at[n, level, h],
            relay_send.at[n, y, h],
            recv_sem.at[n, level, h],
            device_id=(across, lo),
            device_id_type=MESH,
        )

    def send_on(n, first):
        @pl.when(outer)
        def _():
            h = half if first else 1 - half

            def step(y, carry):
                landed = relay.at[n, y, h]
                pltpu.make_async_copy(landed, landed, relay_recv.at[n, y, h]).wait()
                relay_copy(n, y, h).start()
                return carry

            lax.fori_loop(0, half_lats, step, 0)

    def next_step(n):
        def step(k, carry):
            sent_part(n, k)
            send_part(n + AHEAD, k)
            return carry

        lax.fori_loop(0, lons // 2, step, 0)
        send_on(n, True)
        lax.fori_loop(lons // 2, lons, step, 0)
        send_on(n, False)

    def first_part(i, carry):
        send_part(i // lons, lax.rem(i, lons))
        return carry

    lax.fori_loop(0, AHEAD * lons, first_part, 0)

    loads = [
        pltpu.make_async_copy(source, target, weight_sem.at[i])
        for i, (source, target) in enumerate(
            (
                (w_key, key_v),
                (w_value, value_v),
                (w_merge, merge_v),
                (w_qkv, qkv_v),
                (w_out, out_v),
                (w_up, up_v),
                (w_down, down_v),
                (surf, latent.at[0, pl.ds(0, ROWS), pl.ds(0, COLS), :]),
            )
        )
    ]
    for load in loads:
        load.start()
    result[...] = jnp.zeros_like(result)
    latent[:, :, COLS : COLS + GRP, :] = jnp.zeros((LATENT, ROWS + HALO, GRP, D), BF16)
    embed_v[...] = embed_ref[...].astype(F32)

    new = lax.broadcasted_iota(jnp.int32, (D, D), 1)
    old = lax.broadcasted_iota(jnp.int32, (D, D), 0)
    loads[1].wait()
    value_p[...] = dot(
        value_v[...], jnp.where(old == (new % HEADS) * HEAD + new // HEADS, 1.0, 0.0).astype(BF16)
    ).astype(BF16)
    loads[2].wait()
    merge_p[...] = dot(
        jnp.where(new == (old % HEADS) * HEAD + old // HEADS, 1.0, 0.0).astype(BF16), merge_v[...]
    ).astype(BF16)
    loads[0].wait()
    head_of = lax.broadcasted_iota(jnp.int32, (LANES, D), 1) // HEAD
    row_head = lax.broadcasted_iota(jnp.int32, (LANES, D), 0) % HEADS
    for a in range(ATMOS):
        picked = jnp.where(head_of == row_head, queries_ref[a : a + 1, :].astype(F32), 0.0).astype(BF16)
        folded = lax.dot_general(
            picked, key_v[...], (((1,), (1,)), ((), ())), preferred_element_type=F32
        )
        folded = folded.T * (LOG2E / math.sqrt(HEAD))
        fold_v[:, a * LANES : (a + 1) * LANES] = folded.astype(BF16)

    def aggregate(n):
        def landing(i, carry):
            j, h = i // 2, lax.rem(i, 2)
            landed = recv.at[n, j, h]
            pltpu.make_async_copy(landed, landed, recv_sem.at[n, j, h]).wait()
            return carry

        lax.fori_loop(0, 2 * lats, landing, 0)
        for j in range(lats):
            row = embed_v[pl.ds(order_ref[j], 1), :]
            x = recv[n, j].reshape(PATCHES, D).astype(F32) + row
            normed_v[j * PATCHES : (j + 1) * PATCHES, :] = norm(x, kv_gain_ref[...])
        values_v[...] = dot(normed_v[...], value_p[...]).astype(BF16)
        scores_v[...] = dot(normed_v[...], fold_v[...])
        for a in range(ATMOS):
            cut = slice(a * LANES, (a + 1) * LANES)
            level = [scores_v[j * PATCHES : (j + 1) * PATCHES, cut] for j in range(lats)]
            top = functools.reduce(jnp.maximum, level)
            level = [jnp.exp2(s - top) for s in level]
            scale = 1.0 / functools.reduce(jnp.add, level)
            level = [e * scale for e in level]
            for c in range(D // LANES):
                lanes = slice(c * LANES, (c + 1) * LANES)
                mixed = functools.reduce(
                    jnp.add,
                    [
                        level[j] * values_v[j * PATCHES : (j + 1) * PATCHES, lanes].astype(F32)
                        for j in range(lats)
                    ],
                )
                mix_v[a * PATCHES : (a + 1) * PATCHES, lanes] = mixed.astype(BF16)
        merged = dot(mix_v[...], merge_p[...])
        for a in range(ATMOS):
            tokens = merged[a * PATCHES : (a + 1) * PATCHES] + queries_ref[a : a + 1, :].astype(F32)
            tokens = tokens.astype(BF16).reshape(2, SUB, GRP, D)
            for h in range(2):
                first = h * WIN_LAT + n % 2 * SUB
                latent[1 + a, first : first + SUB, n // 2 * GRP : (n // 2 + 1) * GRP, :] = tokens[h]

    def halo(i, levels, rows, cols, to_row, to_col, lat, lon):
        return pltpu.make_async_remote_copy(
            latent.at[pl.ds(*levels), pl.ds(0, rows), pl.ds(cols, GRP), :],
            latent.at[pl.ds(*levels), pl.ds(to_row, rows), pl.ds(to_col, GRP), :],
            halo_send.at[i],
            halo_recv.at[i],
            device_id=(lat, lon),
            device_id_type=MESH,
        )

    every = (0, LATENT)
    row_halos = [halo(g, every, HALO, g * GRP, ROWS, g * GRP, north, lo) for g in range(GROUPS)]

    def packed(cells):
        levels, rows = cells.shape[:2]
        return cells.astype(F32).reshape(levels, rows // 2, GRP, D).astype(BF16)

    def unpacked(cells):
        levels, pairs = cells.shape[:2]
        return cells.astype(F32).reshape(levels, 2 * pairs, EDGE, D).astype(BF16)

    col_halo = pltpu.make_async_remote_copy(
        ahead_out, ahead_in, halo_send.at[4], halo_recv.at[4], device_id=(la, west), device_id_type=MESH
    )
    corner_halo = pltpu.make_async_remote_copy(
        ahead_out.at[:, pl.ds(0, 2), :, :],
        ahead_corner,
        halo_send.at[5],
        halo_recv.at[5],
        device_id=(north, west),
        device_id_type=MESH,
    )

    last = la == lats - 1

    def attend(rw, windows, halfway=None):
        first_row = rw * WIN_LAT + 1
        rows = slice(0, len(windows) * SPAN)

        def place(b, cw):
            return (shift_ref[b, 0] - 1) * 32 + shift_ref[b, 1] + OFFSETS[cw]

        for w, (b, cw) in enumerate(windows):
            cells = latent[pl.ds(2 * b, 2), pl.ds(first_row, 8), BASES[cw] : BASES[cw] + 32, :]
            at = lax.broadcasted_iota(jnp.int32, (SPAN, 512), 1)
            pick = jnp.where(at == to_cells_ref[...] + place(b, cw), 1.0, 0.0).astype(BF16)
            x_v[w * SPAN : (w + 1) * SPAN, :] = dot(pick, cells.reshape(512, D))
        normed = norm(x_v[rows, :], attn_gain_ref[...])
        q_v[rows, :] = (dot(normed, qkv_v[:, :D]) * (LOG2E / math.sqrt(HEAD))).astype(BF16)
        k_v[rows, :] = dot(normed, qkv_v[:, D : 2 * D]).astype(BF16)
        v_v[rows, :] = dot(normed, qkv_v[:, 2 * D :]).astype(BF16)
        lane_head = lax.broadcasted_iota(jnp.int32, (SPAN, LANES), 1) // HEAD
        ones = jnp.ones((SPAN, LANES), BF16)
        row_of_q = lax.broadcasted_iota(jnp.int32, (SPAN, SPAN), 0)
        row_of_k = lax.broadcasted_iota(jnp.int32, (SPAN, SPAN), 1)
        row_of_q = (row_of_q // WIN_LON) % WIN_LAT
        row_of_k = (row_of_k // WIN_LON) % WIN_LAT
        beyond = jnp.where(jnp.logical_and(last, rw == 1), 0, WIN_LAT)

        heads = LANES // HEAD
        own = [lane_head == h for h in range(heads)]

        def window(w, bias):
            at = slice(w * SPAN, (w + 1) * SPAN)
            for c in range(D // LANES):
                lanes = slice(c * LANES, (c + 1) * LANES)
                q = q_v[at, lanes]
                q = jnp.concatenate([jnp.where(own[h], q, jnp.zeros_like(q)) for h in range(heads)], axis=0)
                v = jnp.concatenate([v_v[at, lanes], ones], axis=1)
                s = lax.dot_general(
                    q, k_v[at, lanes], (((1,), (1,)), ((), ())), preferred_element_type=F32
                )
                s = s + bias
                p = jnp.exp2(s - jnp.max(s, axis=-1, keepdims=True)).astype(BF16)
                o = dot(p, v)
                o = o[:, :LANES] * pl.reciprocal(o[:, LANES:], approx=True)
                mixed = o[:SPAN]
                for h in range(1, heads):
                    mixed = jnp.where(own[h], o[h * SPAN : (h + 1) * SPAN], mixed)
                attended_v[at, lanes] = mixed.astype(BF16)

        for b in range(2):
            start = WIN_LAT - shift_ref[b, 0] + beyond
            bias = jnp.where((row_of_q >= start) == (row_of_k >= start), 0.0, -1e30)
            bias = jnp.concatenate([bias] * heads, axis=0)
            for w in range(len(windows)):
                if windows[w][0] == b:
                    window(w, bias)
        if halfway is not None:
            halfway()
        first = (x_v[rows, :] + dot(attended_v[rows, :], out_v[...])).astype(BF16).astype(F32)
        normed = norm(first, mlp_gain_ref[...])
        total = first
        for c in range(FF // 512):
            cut = slice(c * 512, (c + 1) * 512)
            hidden = gelu(dot(normed, up_v[:, cut])).astype(BF16)
            total = total + dot(hidden, down_v[cut, :])
        y_v[rows, :] = total.astype(BF16)
        for w, (b, cw) in enumerate(windows):
            at = lax.broadcasted_iota(jnp.int32, (512, SPAN), 0)
            put = jnp.where(at == from_cells_ref[0:1, :] + place(b, cw), 1.0, 0.0).astype(BF16)
            moved = dot(put, y_v[w * SPAN : (w + 1) * SPAN, :]).astype(BF16).reshape(2, 8, 32, D)
            where = (pl.ds(2 * b, 2), pl.ds(first_row, 8), slice(BASES[cw], BASES[cw] + 32))
            result[where] = result[where] + moved

    def back(i, source, target, lat, lon):
        return pltpu.make_async_remote_copy(
            source, target, back_send.at[i], back_recv.at[i], device_id=(lat, lon), device_id_type=MESH
        )

    def back_south(i, columns):
        return back(
            i,
            result.at[:, pl.ds(ROWS, HALO), pl.ds(*columns), :],
            from_north.at[:, :, pl.ds(*columns), :],
            south,
            lo,
        )

    def back_east(i, pairs):
        return back(i, back_out.at[:, pl.ds(*pairs)], from_west.at[:, pl.ds(*pairs)], la, east)

    def back_pack(first, count):
        back_out[:, first : first + count] = packed(
            result[:, 2 * first : 2 * (first + count), COLS : COLS + EDGE, :]
        )

    backs = (
        back_south(0, (0, GRP)),
        back_south(1, (GRP, COLS - GRP)),
        back(2, back_out.at[:, pl.ds(ROWS // 2, 2)], from_corner, south, east),
        back_east(3, (5, 1)),
        back_east(4, (0, 5)),
    )

    next_step(0)
    aggregate(0)
    loads[7].wait()
    next_step(1)
    aggregate(1)
    ahead_out[...] = packed(latent[:, 0:ROWS, 0:EDGE, :])
    next_step(2)
    aggregate(2)
    next_step(3)
    row_halos[0].start()
    row_halos[1].start()
    corner_halo.start()
    col_halo.start()
    aggregate(3)
    for i in range(3, 7):
        loads[i].wait()

    def first_pair(rw, carry):
        @pl.when(rw == 0)
        def _():
            send_on(4, True)

        @pl.when(rw == 1)
        def _():
            send_on(5, True)
            row_halos[0].wait_recv()
            row_halos[1].wait_recv()

        def halfway():
            @pl.when(rw == 0)
            def _():
                send_on(4, False)

            @pl.when(rw == 1)
            def _():
                send_on(5, False)

        attend(rw, [(b, cw) for b in range(2) for cw in (0, 1)], halfway)
        return carry

    lax.fori_loop(0, 2, first_pair, 0)
    backs[0].start()
    aggregate(4)
    row_halos[2].start()
    col_halo.wait_recv()
    latent[:, 0:ROWS, COLS : COLS + EDGE, :] = unpacked(ahead_in[...])
    corner_halo.wait_recv()
    latent[:, ROWS : ROWS + HALO, COLS : COLS + EDGE, :] = unpacked(ahead_corner[...])[:, :HALO]
    aggregate(5)
    row_halos[2].wait_recv()
    attend(1, [(b, cw) for b in range(2) for cw in (2, 3)])
    backs[1].start()
    back_pack(5, 3)
    backs[2].start()
    backs[3].start()
    attend(0, [(b, 3) for b in range(2)])
    back_pack(0, 5)
    backs[4].start()
    attend(0, [(b, 2) for b in range(2)])

    def finished(b):
        levels = pl.ds(2 * b, 2)
        return pltpu.make_async_copy(
            result.at[levels, pl.ds(0, ROWS), pl.ds(0, COLS), :], out.at[levels], out_sem.at[b]
        )

    for copy in backs:
        copy.wait_recv()
    for b in range(2):
        levels = slice(2 * b, 2 * b + 2)
        result[levels, 0:HALO, 0:COLS, :] = result[levels, 0:HALO, 0:COLS, :] + from_north[levels]
        result[levels, 0:ROWS, 0:EDGE, :] = result[levels, 0:ROWS, 0:EDGE, :] + unpacked(from_west[levels])
        result[levels, 0:HALO, 0:EDGE, :] = (
            result[levels, 0:HALO, 0:EDGE, :] + unpacked(from_corner[levels])[:, :HALO]
        )
        finished(b).start()
    for copy in backs:
        copy.wait_send()
    for copy in row_halos + [col_halo, corner_halo]:
        copy.wait_send()

    def sent(i, carry):
        sent_part(STEPS - AHEAD + i // lons, lax.rem(i, lons))
        return carry

    lax.fori_loop(0, AHEAD * lons, sent, 0)

    @pl.when(outer)
    def _():
        def step(i, carry):
            relay_copy(i // lats, lax.rem(i, lats) // 2, lax.rem(i, 2)).wait_send()
            return carry

        lax.fori_loop(0, STEPS * lats, step, 0)

    for b in range(2):
        finished(b).wait()


def shards(
    lats,
    lons,
    level_slabs,
    surf_tokens,
    level_order,
    level_embed,
    kv_gain,
    latent_queries,
    w_key,
    w_value,
    w_merge,
    attn_gain,
    w_qkv,
    w_out,
    mlp_gain,
    w_up,
    w_down,
    window_shift,
):
    token = np.arange(SPAN)
    cell = (token // 72) * 256 + (token % 72) // 12 * 32 + token % 12
    to_cells = jnp.asarray(cell[:, None], jnp.int32)
    from_cells = jnp.asarray(np.broadcast_to(cell[None, :], (8, SPAN)), jnp.int32)
    smem = pl.BlockSpec(memory_space=pltpu.SMEM)
    vmem = pl.BlockSpec(memory_space=pltpu.VMEM)
    hbm = pl.BlockSpec(memory_space=pl.ANY)
    tokens = lats * PATCHES
    return pl.pallas_call(
        functools.partial(kernel, lats, lons),
        out_shape=jax.ShapeDtypeStruct((LATENT, ROWS, COLS, D), BF16),
        in_specs=[smem] * 2 + [hbm] * 2 + [vmem] * 7 + [hbm] * 7,
        out_specs=hbm,
        scratch_shapes=[
            pltpu.VMEM((STEPS, lats, 2, SUB, GRP, D), BF16),
            pltpu.VMEM((STEPS, lats // 2, 2, SUB, GRP, D), BF16),
            pltpu.VMEM((LATENT, ROWS + HALO, COLS + GRP, D), BF16),
            pltpu.VMEM((LATENT, ROWS + HALO + 1, COLS + GRP, D), BF16),
            pltpu.VMEM((LATENT, HALO, COLS, D), BF16),
            pltpu.VMEM((LATENT, ROWS // 2, GRP, D), BF16),
            pltpu.VMEM((LATENT, 2, GRP, D), BF16),
            pltpu.VMEM((LATENT, ROWS // 2, GRP, D), BF16),
            pltpu.VMEM((LATENT, ROWS // 2, GRP, D), BF16),
            pltpu.VMEM((LATENT, 2, GRP, D), BF16),
            pltpu.VMEM((LATENT, ROWS // 2 + 2, GRP, D), BF16),
            pltpu.VMEM((D, D), BF16),
            pltpu.VMEM((D, D), BF16),
            pltpu.VMEM((D, D), BF16),
            pltpu.VMEM((D, 3 * D), BF16),
            pltpu.VMEM((D, D), BF16),
            pltpu.VMEM((D, FF), BF16),
            pltpu.VMEM((FF, D), BF16),
            pltpu.VMEM((lats, D), F32),
            pltpu.VMEM((D, ATMOS * LANES), BF16),
            pltpu.VMEM((D, D), BF16),
            pltpu.VMEM((D, D), BF16),
            pltpu.VMEM((tokens, D), BF16),
            pltpu.VMEM((tokens, D), BF16),
            pltpu.VMEM((tokens, ATMOS * LANES), F32),
            pltpu.VMEM((ATMOS * PATCHES, D), BF16),
            pltpu.VMEM((BATCH, D), F32),
            pltpu.VMEM((BATCH, D), BF16),
            pltpu.VMEM((BATCH, D), BF16),
            pltpu.VMEM((BATCH, D), BF16),
            pltpu.VMEM((BATCH, D), BF16),
            pltpu.VMEM((BATCH, D), BF16),
            pltpu.SemaphoreType.DMA((STEPS, lons)),
            pltpu.SemaphoreType.DMA((STEPS, lats, 2)),
            pltpu.SemaphoreType.DMA((STEPS, lats // 2, 2)),
            pltpu.SemaphoreType.DMA((STEPS, lats // 2, 2)),
            pltpu.SemaphoreType.DMA((8,)),
            pltpu.SemaphoreType.DMA((6,)),
            pltpu.SemaphoreType.DMA((6,)),
            pltpu.SemaphoreType.DMA((5,)),
            pltpu.SemaphoreType.DMA((5,)),
            pltpu.SemaphoreType.DMA((2,)),
        ],
        compiler_params=pltpu.CompilerParams(
            collective_id=0, has_side_effects=True, vmem_limit_bytes=56 * 1024 * 1024
        ),
        name="encoder",
    )(
        level_order,
        window_shift,
        level_slabs,
        surf_tokens,
        level_embed,
        kv_gain.reshape(1, D),
        latent_queries,
        attn_gain.reshape(1, D),
        mlp_gain.reshape(1, D),
        to_cells,
        from_cells,
        w_key,
        w_value,
        w_merge,
        w_qkv,
        w_out,
        w_up,
        w_down,
    )


def solution(mesh):
    in_specs = (P("lat", "lon", None, None), P("lat", "lon", None)) + (P(),) * 14
    return jax.shard_map(
        functools.partial(shards, mesh.shape["lat"], mesh.shape["lon"]),
        mesh=mesh,
        in_specs=in_specs,
        out_specs=P(None, "lat", "lon", None),
        check_vma=False,
    )
```
